256 devices in a mesh: emx: 8 (over y, x_hi), emy: 16 (over z, core), grp: 2 (over x_lo).
Axes of the slice: x: 4 (x_hi: 2, x_lo: 2; x = x_hi * 2 + x_lo), y: 4, z: 8, core: 2. Of those that a mesh axis runs over, the one named last changes fastest.
Arguments:
- efield: float32 [3, 12, 256, 4096], P(None, None, 'emx', ('emy', 'grp')), may hold values from -6 to 6
- hfield: float32 [3, 12, 256, 4096], P(None, None, 'emx', ('emy', 'grp')), may hold values from -6 to 6
- magnet: float32 [3, 8, 256, 4096], P(None, None, ('emx', 'emy', 'grp')), may hold values from -6 to 6
- material: int32 [256, 4096], P('emx', ('emy', 'grp')), may hold values from 0 to 3
- drive: float32 [256, 4096], P('emx', ('emy', 'grp')), may hold values from -6 to 6
Outputs:
- efield_new: float32 [3, 12, 256, 4096], P(None, None, 'emx', ('emy', 'grp'))
- hfield_new: float32 [3, 12, 256, 4096], P(None, None, 'emx', ('emy', 'grp'))
- magnet_new: float32 [3, 8, 256, 4096], P(None, None, ('emx', 'emy', 'grp'))
The draws below stay inside these ranges and needn't reach their ends.
All inputs are finite; a program needn't handle non-finite values.
Results may differ from the reference program's by a relative error of at most 0.00002.
Values sent between devices are 32-bit elements; how exact they have to be, the bound alone decides.
A program may use at most 64 MiB of HBM per device.

```python
import jax
import jax.numpy as jnp
from jax import lax

NZ = 12
FZ = 8
W = 8
NX = 256
NY = 4096


def place_ends(result, stream_key, low, largest):
    place = [jax.random.randint(jax.random.fold_in(stream_key, axis), (), 0, length) for axis, length in enumerate(result.shape)]
    widest = result.shape.index(max(result.shape))
    next_to = place[:widest] + [(place[widest] + 1) % result.shape[widest]] + place[widest + 1:]
    return result.at[tuple(place)].set(low).at[tuple(next_to)].set(largest)


def levels(own_key, extent, pieces, smallest, largest):
    def one(axis_at, blocks):
        draws = jax.random.uniform(jax.random.fold_in(jax.random.fold_in(own_key, 6), axis_at), (blocks,), jnp.float32, smallest / len(pieces), largest / len(pieces))
        return jnp.repeat(jnp.exp(draws), extent[axis_at] // blocks).reshape((-1,) + (1,) * (len(extent) - axis_at - 1))

    factor_of = one(*pieces[0])
    for cut in pieces[1:]:
        factor_of = factor_of * one(*cut)
    return factor_of


def centred(key, shape, width, most, shards=(), held_as=jnp.bfloat16):
    entries = width * jax.random.normal(key, shape, jnp.float32)
    if shards:
        entries = entries * levels(key, shape, shards, -0.22, 0.18)
    return jnp.clip(entries, -most, most).astype(held_as)


def setup_inputs(seed: int = 0) -> dict:
    seeds = jax.random.split(jax.random.key(seed), 6)
    return {
        "efield": centred(seeds[0], (3, NZ, NX, NY), 1.0, 6.0, ((2, 8), (3, 32)), jnp.float32),
        "hfield": centred(seeds[1], (3, NZ, NX, NY), 1.0, 6.0, ((2, 8), (3, 32)), jnp.float32),
        "magnet": centred(seeds[2], (3, FZ, NX, NY), 1.0, 6.0, ((2, 256),), jnp.float32),
        "material": place_ends(jax.random.randint(seeds[3], (NX, NY), 0, 4), jax.random.fold_in(seeds[3], 1), 0, 3).astype(jnp.int32),
        "drive": centred(seeds[4], (NX, NY), 1.0, 6.0, ((0, 8), (1, 32)), jnp.float32),
    }


step_dt = 0.5
film_eps = 15.0
exch_coef = 0.25
gyro_coef = 0.3
damp_coef = 0.1


def grade(index, count):
    edge = jnp.minimum(index, count - 1 - index)
    depth = jnp.maximum(W - edge, 0).astype(jnp.float32) / W
    return 0.4 * depth * depth


def lower_diff(field, along):
    widths = [(0, 0)] * field.ndim
    widths[along] = (1, 0)
    padded = jnp.pad(field, widths)
    return field - lax.slice_in_dim(padded, 0, field.shape[along], axis=along)


def upper_diff(field, along):
    widths = [(0, 0)] * field.ndim
    widths[along] = (0, 1)
    padded = jnp.pad(field, widths)
    return lax.slice_in_dim(padded, 1, field.shape[along] + 1, axis=along) - field


def cross_product(left, right):
    return jnp.stack([left[1] * right[2] - left[2] * right[1],
                      left[2] * right[0] - left[0] * right[2],
                      left[0] * right[1] - left[1] * right[0]])


def permittivity(material, layers):
    upper_eps = jnp.where(material == 0, 1.0, jnp.where(material == 1, 2.2, jnp.where(material == 2, 4.4, 9.8))).astype(jnp.float32)
    layer_index = lax.broadcasted_iota(jnp.int32, (layers, 1, 1), 0)
    return jnp.where(layer_index < FZ, jnp.float32(film_eps), upper_eps[None])


def spin_step(spins, field_film, lateral):
    zpadded = jnp.pad(spins, ((0, 0), (1, 1), (0, 0), (0, 0)))
    laplace = lateral + zpadded[:, 2:] + zpadded[:, :-2] - 6.0 * spins
    effective = field_film + exch_coef * laplace
    effective = jnp.stack([effective[0], effective[1], effective[2] + 1.0 + 0.5 * spins[2]])
    torque = cross_product(spins, effective)
    return spins - gyro_coef * (torque + damp_coef * cross_product(spins, torque))


def advance_fields(efield, hfield, material, drive, index_x, index_y, count_x, count_y, diff_b, diff_f):
    layers = efield.shape[1]
    sigma = grade(index_x, count_x)[:, None] + grade(index_y, count_y)[None, :]
    decay = (1.0 - sigma) / (1.0 + sigma)
    estep = step_dt / (permittivity(material, layers) * (1.0 + sigma))
    hstep = step_dt / (1.0 + sigma)
    layer_index = lax.broadcasted_iota(jnp.int32, (layers, 1, 1), 0)
    source = jnp.where(layer_index == layers - 1, drive[None], jnp.float32(0.0))
    comp_x = diff_b(hfield, 2, 2) - lower_diff(hfield[1], 0) - source
    comp_y = lower_diff(hfield[0], 0) - diff_b(hfield, 2, 1)
    comp_z = diff_b(hfield, 1, 1) - diff_b(hfield, 0, 2)
    efield_new = jnp.stack([decay * efield[0] + estep * comp_x,
                            decay * efield[1] + estep * comp_y,
                            decay * efield[2] + estep * comp_z])
    curl_x = diff_f(efield_new, 2, 2) - upper_diff(efield_new[1], 0)
    curl_y = upper_diff(efield_new[0], 0) - diff_f(efield_new, 2, 1)
    curl_z = diff_f(efield_new, 1, 1) - diff_f(efield_new, 0, 2)
    hhalf = jnp.stack([decay * hfield[0] - hstep * curl_x,
                       decay * hfield[1] - hstep * curl_y,
                       decay * hfield[2] - hstep * curl_z])
    return efield_new, hhalf


def reference(efield, hfield, magnet, material, drive):
    index_x = lax.iota(jnp.int32, NX)
    index_y = lax.iota(jnp.int32, NY)

    def diff_b(field, comp, along):
        return lower_diff(field[comp], along)

    def diff_f(field, comp, along):
        return upper_diff(field[comp], along)

    efield_new, hhalf = advance_fields(efield, hfield, material, drive, index_x, index_y, NX, NY, diff_b, diff_f)
    padded = jnp.pad(magnet, ((0, 0), (0, 0), (1, 1), (1, 1)))
    lateral = padded[:, :, 2:, 1:-1] + padded[:, :, :-2, 1:-1] + padded[:, :, 1:-1, 2:] + padded[:, :, 1:-1, :-2]
    magnet_new = spin_step(magnet, hhalf[:, :FZ], lateral)
    hfield_new = jnp.concatenate([hhalf[:, :FZ] - (magnet_new - magnet), hhalf[:, FZ:]], axis=1)
    return efield_new, hfield_new, magnet_new
```

```python
import functools

import jax
import jax.numpy as jnp
from jax import lax
from jax.experimental import pallas as pl
from jax.experimental.pallas import tpu as pltpu
from jax.sharding import PartitionSpec as P

FZ = 8
W = 8

step_dt = 0.5
film_eps = 15.0
exch_coef = 0.25
gyro_coef = 0.3
damp_coef = 0.1

MESH = pl.DeviceIdType.MESH
LANES = 128
TILE = 8


def grade(index, count):
    edge = jnp.minimum(index, count - 1 - index)
    depth = jnp.maximum(W - edge, 0).astype(jnp.float32) / W
    return 0.4 * depth * depth


def spread_order(count):
    half = count // 2
    order = [half]
    for step in range(1, half):
        order += [half + step, half - step]
    return order


def step_kernel(
    sizes,
    e_in, h_in, m_in, mat_in, drv_in,
    e_out, h_out, m_out,
    e, h, m, mat, drv,
    chunk, cols, got, got_cols,
    hx_send, hx_got, hy_send, hy_got,
    ex_send, ex_got, ey_send, ey_got,
    back, back_got,
    load_sem, store_sem, own_sem,
    send_sem, halo_sem, chunk_sem, cols_sem, edge_sem, back_sem,
):
    nz, rows, count_x, group, emy, grp = sizes
    tiles = rows // TILE
    film = 3 * FZ
    a = lax.axis_index("emx")
    b = lax.axis_index("emy") * grp + lax.axis_index("grp")

    def peer(index):
        return {"emx": a, "emy": index // grp, "grp": lax.rem(index, grp)}

    a_next, a_prev = lax.rem(a + 1, count_x), lax.rem(a + count_x - 1, count_x)
    b_next, b_prev = lax.rem(b + 1, group), lax.rem(b + group - 1, group)
    to_a_next, to_a_prev = {"emx": a_next}, {"emx": a_prev}
    order = spread_order(group)

    loads = [
        pltpu.make_async_copy(src, dst, load_sem.at[i])
        for i, (src, dst) in enumerate(
            ((m_in, m), (h_in, h), (e_in, e), (mat_in, mat), (drv_in, drv))
        )
    ]
    for load in loads:
        load.start()

    barrier = pltpu.get_barrier_semaphore()
    for k in order:
        pl.semaphore_signal(
            barrier, inc=1, device_id=peer(lax.rem(b + k, group)), device_id_type=MESH
        )
    for device in (to_a_next, to_a_prev):
        pl.semaphore_signal(barrier, inc=1, device_id=device, device_id_type=MESH)

    lane = lax.broadcasted_iota(jnp.int32, (TILE, LANES), 1)

    def column(tile, at):
        return jnp.broadcast_to(tile[:, at : at + 1], (TILE, LANES))

    loads[0].wait()
    lasts, firsts = [], []
    for t in range(tiles):
        last = jnp.zeros((TILE, LANES), jnp.float32)
        first = jnp.zeros((TILE, LANES), jnp.float32)
        for q in range(film):
            v = m[pl.ds(q * rows + t * TILE, TILE), :]
            chunk[pl.ds(t * TILE * film + q, TILE, stride=film), :] = v
            last = jnp.where(lane == q, column(v, LANES - 1), last)
            first = jnp.where(lane == film + q, column(v, 0), first)
        lasts.append(last)
        firsts.append(first)
    last = jnp.concatenate(lasts, axis=0)
    first = jnp.concatenate(firsts, axis=0)
    wide = lax.broadcasted_iota(jnp.int32, (rows, LANES), 1)
    deep = lax.broadcasted_iota(jnp.int32, (rows, LANES), 0)
    last = jnp.where(deep == 0, 0.0, pltpu.roll(last, 1, 0))
    first = jnp.where(deep == rows - 1, 0.0, pltpu.roll(first, rows - 1, 0))
    cols[...] = jnp.where(wide < film, last, first).reshape(rows, 1, LANES)

    def field(ref, comp, z):
        return ref[pl.ds((comp * nz + z) * rows, rows), :]

    def tile_of(ref, comp, z, t):
        return ref[pl.ds((comp * nz + z) * rows + t * TILE, TILE), :]

    def pack(ref, comps, at):
        packed = jnp.zeros((TILE, LANES), jnp.float32)
        for n, comp in enumerate(comps):
            for z in range(nz):
                for t in range(tiles):
                    v = tile_of(ref, comp, z, t)
                    packed = jnp.where(
                        lane == (n * nz + z) * tiles + t, column(v, at), packed
                    )
        return packed

    def unpack(packed, n, z):
        first = (n * nz + z) * tiles
        return jnp.concatenate([column(packed, first + t) for t in range(tiles)], axis=0)

    loads[1].wait()
    for n, comp in enumerate((1, 2)):
        hx_send[pl.ds(n * nz, nz), :] = h[
            pl.ds(comp * nz * rows + rows - 1, nz, stride=rows), :
        ]
    hy_send[...] = pack(h, (0, 2), LANES - 1)

    pl.semaphore_wait(barrier, group + 1)

    def send(src, dst, sem, device):
        copy = pltpu.make_async_remote_copy(
            src_ref=src,
            dst_ref=dst,
            send_sem=send_sem.at[0],
            recv_sem=sem,
            device_id=device,
            device_id_type=MESH,
        )
        copy.start()
        return copy

    def halo(src, dst, which, device):
        copy = pltpu.make_async_remote_copy(
            src_ref=src,
            dst_ref=dst,
            send_sem=halo_sem.at[0, which],
            recv_sem=halo_sem.at[1, which],
            device_id=device,
            device_id_type=MESH,
        )
        copy.start()
        return copy

    hx = halo(hx_send, hx_got, 0, to_a_next)
    hy = halo(hy_send, hy_got, 1, peer(b_next))
    mine = b // TILE
    own = [
        pltpu.make_async_copy(
            chunk.at[pl.ds(pl.multiple_of(b * film, film), film)],
            got.at[pl.ds(pl.multiple_of((b + 1) * film, film), film)],
            chunk_sem.at[mine],
        ),
        pltpu.make_async_copy(cols.at[b], got_cols.at[b], cols_sem.at[mine]),
    ]
    for copy in own:
        copy.start()
    for k in order:
        j = lax.rem(b + k, group)
        send(
            chunk.at[pl.ds(pl.multiple_of(j * film, film), film)],
            got.at[pl.ds(pl.multiple_of((b + 1) * film, film), film)],
            chunk_sem.at[mine],
            peer(j),
        )
        pltpu.make_async_remote_copy(
            src_ref=cols.at[j],
            dst_ref=got_cols.at[b],
            send_sem=send_sem.at[1],
            recv_sem=cols_sem.at[mine],
            device_id=peer(j),
            device_id_type=MESH,
        ).start()

    for load in loads[2:]:
        load.wait()
    index_x = a * rows + lax.broadcasted_iota(jnp.int32, (rows, LANES), 0)
    index_y = b * LANES + lax.broadcasted_iota(jnp.int32, (rows, LANES), 1)
    sigma = grade(index_x, count_x * rows) + grade(index_y, group * LANES)
    decay = (1.0 - sigma) / (1.0 + sigma)
    hstep = step_dt / (1.0 + sigma)
    film_step = step_dt / (film_eps * (1.0 + sigma))
    material = mat[...]
    eps = jnp.where(
        material == 0, 1.0, jnp.where(material == 1, 2.2, jnp.where(material == 2, 4.4, 9.8))
    ).astype(jnp.float32)
    upper_step = step_dt / (eps * (1.0 + sigma))

    hx.wait()
    hy.wait()
    left = jnp.where(b == 0, 0.0, hy_got[...])

    def below_x(v, n, z):
        edge = jnp.where(a == 0, 0.0, hx_got[pl.ds(n * nz + z, 1), :])
        return jnp.where(deep == 0, edge, pltpu.roll(v, 1, 0))

    def below_y(v, n, z):
        return jnp.where(wide == 0, unpack(left, n, z), pltpu.roll(v, 1, 1))

    under = None
    for z in range(nz):
        hx_z, hy_z, hz_z = (field(h, comp, z) for comp in range(3))
        back_zy = hz_z - below_y(hz_z, 1, z)
        back_zx = hz_z - below_x(hz_z, 1, z)
        back_yx = hy_z - below_x(hy_z, 0, z)
        back_xy = hx_z - below_y(hx_z, 0, z)
        back_yz = hy_z if under is None else hy_z - under[1]
        back_xz = hx_z if under is None else hx_z - under[0]
        comp_x = back_zy - back_yz
        if z == nz - 1:
            comp_x = comp_x - drv[...]
        comp_y = back_xz - back_zx
        comp_z = back_yx - back_xy
        estep = film_step if z < FZ else upper_step
        for comp, value in enumerate((comp_x, comp_y, comp_z)):
            e[pl.ds((comp * nz + z) * rows, rows), :] = decay * field(e, comp, z) + estep * value
        under = (hx_z, hy_z)

    for n, comp in enumerate((1, 2)):
        ex_send[pl.ds(n * nz, nz), :] = e[pl.ds(comp * nz * rows, nz, stride=rows), :]
    ey_send[...] = pack(e, (0, 2), 0)
    ex = halo(ex_send, ex_got, 2, to_a_prev)
    ey = halo(ey_send, ey_got, 3, peer(b_prev))
    e_store = pltpu.make_async_copy(e, e_out, store_sem.at[0])
    e_store.start()

    ex.wait()
    ey.wait()
    right = jnp.where(b == group - 1, 0.0, ey_got[...])

    def above_x(v, n, z):
        edge = jnp.where(a == count_x - 1, 0.0, ex_got[pl.ds(n * nz + z, 1), :])
        return jnp.where(deep == rows - 1, edge, pltpu.roll(v, rows - 1, 0))

    def above_y(v, n, z):
        return jnp.where(wide == LANES - 1, unpack(right, n, z), pltpu.roll(v, LANES - 1, 1))

    for z in range(nz):
        ex_z, ey_z, ez_z = (field(e, comp, z) for comp in range(3))
        fore_zy = above_y(ez_z, 1, z) - ez_z
        fore_zx = above_x(ez_z, 1, z) - ez_z
        fore_yx = above_x(ey_z, 0, z) - ey_z
        fore_xy = above_y(ex_z, 0, z) - ex_z
        fore_yz = (field(e, 1, z + 1) if z < nz - 1 else 0.0) - ey_z
        fore_xz = (field(e, 0, z + 1) if z < nz - 1 else 0.0) - ex_z
        curls = (fore_zy - fore_yz, fore_xz - fore_zx, fore_yx - fore_xy)
        for comp, value in enumerate(curls):
            h[pl.ds((comp * nz + z) * rows, rows), :] = decay * field(h, comp, z) - hstep * value

    def rows_of(first, n):
        return got.at[pl.ds(first * film, n * film)]

    def wait_group(t):
        pltpu.make_async_copy(
            rows_of(1 + t * TILE, TILE), rows_of(1 + t * TILE, TILE), chunk_sem.at[t]
        ).wait()
        pltpu.make_async_copy(
            got_cols.at[pl.ds(t * TILE, TILE)], got_cols.at[pl.ds(t * TILE, TILE)], cols_sem.at[t]
        ).wait()

    def edge(src, dst, which, device):
        copy = pltpu.make_async_remote_copy(
            src_ref=rows_of(src, 1),
            dst_ref=rows_of(dst, 1),
            send_sem=edge_sem.at[0, which],
            recv_sem=edge_sem.at[1, which],
            device_id=device,
            device_id_type=MESH,
        )
        copy.start()
        return copy

    wait_group(0)
    low = edge(1, rows + 1, 0, to_a_prev)
    for t in range(1, tiles):
        wait_group(t)
    high = edge(rows, 0, 1, to_a_next)

    def spin(t):
        sides = got_cols[pl.ds(t * TILE, TILE)].reshape(TILE, LANES)

        def spins(comp, z, shift):
            first = (t * TILE + 1 + shift) * film + comp * FZ + z
            return got[pl.ds(first, TILE, stride=film), :]

        for z in range(FZ):
            centre = [spins(comp, z, 0) for comp in range(3)]
            heff = []
            for comp in range(3):
                v = centre[comp]
                q = comp * FZ + z
                y_up = jnp.where(
                    lane == LANES - 1, column(sides, film + q), pltpu.roll(v, LANES - 1, 1)
                )
                y_down = jnp.where(lane == 0, column(sides, q), pltpu.roll(v, 1, 1))
                lap = spins(comp, z, 1) + spins(comp, z, -1) + y_up + y_down
                if z < FZ - 1:
                    lap = lap + spins(comp, z + 1, 0)
                if z > 0:
                    lap = lap + spins(comp, z - 1, 0)
                lap = lap - 6.0 * v
                value = tile_of(h, comp, z, t) + exch_coef * lap
                if comp == 2:
                    value = value + 1.0 + 0.5 * v
                heff.append(value)
            mx, my, mz = centre
            tx = my * heff[2] - mz * heff[1]
            ty = mz * heff[0] - mx * heff[2]
            tz = mx * heff[1] - my * heff[0]
            dx = -gyro_coef * (tx + damp_coef * (my * tz - mz * ty))
            dy = -gyro_coef * (ty + damp_coef * (mz * tx - mx * tz))
            dz = -gyro_coef * (tz + damp_coef * (mx * ty - my * tx))
            for comp, d in enumerate((dx, dy, dz)):
                at = pl.ds((comp * nz + z) * rows + t * TILE, TILE)
                h[at, :] = h[at, :] - d
            big_x, big_y = largest(mx, my, mz)
            u = jnp.where(big_x, dy, jnp.where(big_y, dz, dx))
            v = jnp.where(big_x, dz, jnp.where(big_y, dx, dy))
            back[pl.ds(t * TILE * 2 * FZ + z, TILE, stride=2 * FZ), :] = u
            back[pl.ds(t * TILE * 2 * FZ + FZ + z, TILE, stride=2 * FZ), :] = v

    def part(ref, index):
        return ref.at[pl.ds(pl.multiple_of(index * 2 * FZ, 2 * FZ), 2 * FZ)]

    def send_back(t):
        for i in range(t * TILE, (t + 1) * TILE):

            @pl.when(b != i)
            def _():
                pltpu.make_async_remote_copy(
                    src_ref=part(back, i),
                    dst_ref=part(back_got, b),
                    send_sem=send_sem.at[2],
                    recv_sem=back_sem.at[mine],
                    device_id={"emx": a, "emy": i // grp, "grp": i % grp},
                    device_id_type=MESH,
                ).start()

            @pl.when(b == i)
            def _():
                pltpu.make_async_copy(part(back, i), part(back_got, b), back_sem.at[mine]).start()

    for t in range(1, tiles - 1):
        spin(t)
        send_back(t)

    low.wait()
    high.wait()

    @pl.when(a == 0)
    def _():
        got[pl.ds(0, film), :] = jnp.zeros((film, LANES), jnp.float32)

    @pl.when(a == count_x - 1)
    def _():
        got[pl.ds((rows + 1) * film, film), :] = jnp.zeros((film, LANES), jnp.float32)

    for t in sorted({0, tiles - 1}):
        spin(t)
        send_back(t)
    h_store = pltpu.make_async_copy(h, h_out, store_sem.at[1])
    h_store.start()

    for t in range(tiles):
        landed = back_got.at[pl.ds(t * TILE * 2 * FZ, TILE * 2 * FZ)]
        pltpu.make_async_copy(landed, landed, back_sem.at[t]).wait()
        for z in range(FZ):
            places = [pl.ds((comp * FZ + z) * rows + t * TILE, TILE) for comp in range(3)]
            mx, my, mz = (m[at, :] for at in places)
            u = back_got[pl.ds(t * TILE * 2 * FZ + z, TILE, stride=2 * FZ), :]
            v = back_got[pl.ds(t * TILE * 2 * FZ + FZ + z, TILE, stride=2 * FZ), :]
            big_x, big_y = largest(mx, my, mz)
            big = jnp.where(big_x, mx, jnp.where(big_y, my, mz))
            mu = jnp.where(big_x, my, jnp.where(big_y, mz, mx))
            mv = jnp.where(big_x, mz, jnp.where(big_y, mx, my))
            tiny = jnp.abs(big) < 1e-30
            scale = jnp.where(tiny, 0.0, 1.0 / jnp.where(tiny, 1.0, big))
            w = -((mu * scale) * u + (mv * scale) * v)
            m[places[0], :] = mx + jnp.where(big_x, w, jnp.where(big_y, v, u))
            m[places[1], :] = my + jnp.where(big_x, u, jnp.where(big_y, w, v))
            m[places[2], :] = mz + jnp.where(big_x, v, jnp.where(big_y, u, w))
    m_store = pltpu.make_async_copy(m, m_out, store_sem.at[2])
    m_store.start()

    for ref, sem in ((chunk, 0), (back, 2)):
        size = ref.shape[0] // group * (group - 1)
        sent = ref.at[pl.ds(0, size)]
        pltpu.make_async_copy(sent, sent, send_sem.at[sem]).wait()
    sent = cols.at[pl.ds(0, group - 1)]
    pltpu.make_async_copy(sent, sent, send_sem.at[1]).wait()
    e_store.wait()
    h_store.wait()
    m_store.wait()


def largest(mx, my, mz):
    sx, sy, sz = jnp.abs(mx), jnp.abs(my), jnp.abs(mz)
    big_x = (sx >= sy) & (sx >= sz)
    big_y = sy >= sz
    return big_x, big_y


def shards(efield, hfield, magnet, material, drive):
    _, nz, rows, cols_y = efield.shape
    count_x = lax.axis_size("emx")
    emy, grp = lax.axis_size("emy"), lax.axis_size("grp")
    group = emy * grp
    assert cols_y == LANES and rows == group and magnet.shape[2] == 1
    film = 3 * FZ
    tiles = rows // TILE
    assert 2 * nz * tiles <= LANES and 2 * film <= LANES
    f32 = jnp.float32
    field_shape = (3 * nz * rows, LANES)
    spin_shape = (film * group, LANES)
    dma = pltpu.SemaphoreType.DMA
    any_spec = pl.BlockSpec(memory_space=pl.ANY)
    sizes = (nz, rows, count_x, group, emy, grp)
    outs = pl.pallas_call(
        functools.partial(step_kernel, sizes),
        out_shape=(
            jax.ShapeDtypeStruct(field_shape, f32),
            jax.ShapeDtypeStruct(field_shape, f32),
            jax.ShapeDtypeStruct(spin_shape, f32),
        ),
        in_specs=[any_spec] * 5,
        out_specs=[any_spec] * 3,
        scratch_shapes=[
            pltpu.VMEM(field_shape, f32),
            pltpu.VMEM(field_shape, f32),
            pltpu.VMEM(spin_shape, f32),
            pltpu.VMEM((rows, LANES), jnp.int32),
            pltpu.VMEM((rows, LANES), f32),
            pltpu.VMEM((group * film, LANES), f32),
            pltpu.VMEM((group, 1, LANES), f32),
            pltpu.VMEM(((rows + 2) * film, LANES), f32),
            pltpu.VMEM((rows, 1, LANES), f32),
            pltpu.VMEM((2 * nz, LANES), f32),
            pltpu.VMEM((2 * nz, LANES), f32),
            pltpu.VMEM((TILE, LANES), f32),
            pltpu.VMEM((TILE, LANES), f32),
            pltpu.VMEM((2 * nz, LANES), f32),
            pltpu.VMEM((2 * nz, LANES), f32),
            pltpu.VMEM((TILE, LANES), f32),
            pltpu.VMEM((TILE, LANES), f32),
            pltpu.VMEM((rows * 2 * FZ, LANES), f32),
            pltpu.VMEM((group * 2 * FZ, LANES), f32),
            dma((5,)),
            dma((3,)),
            dma((1,)),
            dma((3,)),
            dma((2, 4)),
            dma((tiles,)),
            dma((tiles,)),
            dma((2, 2)),
            dma((tiles,)),
        ],
        compiler_params=pltpu.CompilerParams(
            collective_id=0, has_side_effects=True, vmem_limit_bytes=32 * 1024 * 1024
        ),
    )(
        efield.reshape(field_shape),
        hfield.reshape(field_shape),
        magnet.reshape(spin_shape),
        material,
        drive,
    )
    return (
        outs[0].reshape(efield.shape),
        outs[1].reshape(hfield.shape),
        outs[2].reshape(magnet.shape),
    )


def solution(mesh):
    return jax.shard_map(
        shards,
        mesh=mesh,
        in_specs=(
            P(None, None, "emx", ("emy", "grp")),
            P(None, None, "emx", ("emy", "grp")),
            P(None, None, ("emx", "emy", "grp"), None),
            P("emx", ("emy", "grp")),
            P("emx", ("emy", "grp")),
        ),
        out_specs=(
            P(None, None, "emx", ("emy", "grp")),
            P(None, None, "emx", ("emy", "grp")),
            P(None, None, ("emx", "emy", "grp"), None),
        ),
        check_vma=False,
    )
```

```python
import functools

import jax
import jax.numpy as jnp
from jax import lax
from jax.experimental import pallas as pl
from jax.experimental.pallas import tpu as pltpu
from jax.sharding import PartitionSpec as P

FZ = 8
W = 8

step_dt = 0.5
film_eps = 15.0
exch_coef = 0.25
gyro_coef = 0.3
damp_coef = 0.1

MESH = pl.DeviceIdType.MESH
LANES = 128
TILE = 8


def grade(index, count):
    edge = jnp.minimum(index, count - 1 - index)
    depth = jnp.maximum(W - edge, 0).astype(jnp.float32) / W
    return 0.4 * depth * depth


def spread_order(count):
    half = count // 2
    order = [half]
    for step in range(1, half):
        order += [half + step, half - step]
    return order


def step_kernel(
    sizes,
    e_in, h_in, m_in, mat_in, drv_in,
    e, h, m,
    mat, drv,
    chunk, cols, got, got_cols,
    hx_send, hx_got, hy_send, hy_got,
    ex_send, ex_got, ey_send, ey_got,
    back, back_got,
    load_sem,
    send_sem, halo_sem, chunk_sem, cols_sem, edge_sem, back_sem,
):
    nz, rows, count_x, group, emy, grp = sizes
    tiles = rows // TILE
    film = 3 * FZ
    a = lax.axis_index("emx")
    b = lax.axis_index("emy") * grp + lax.axis_index("grp")

    def peer(index):
        return {"emx": a, "emy": index // grp, "grp": lax.rem(index, grp)}

    a_next, a_prev = lax.rem(a + 1, count_x), lax.rem(a + count_x - 1, count_x)
    b_next, b_prev = lax.rem(b + 1, group), lax.rem(b + group - 1, group)
    to_a_next, to_a_prev = {"emx": a_next}, {"emx": a_prev}
    order = spread_order(group)

    loads = [
        pltpu.make_async_copy(src, dst, load_sem.at[i])
        for i, (src, dst) in enumerate(
            ((m_in, m), (h_in, h), (e_in, e), (mat_in, mat), (drv_in, drv))
        )
    ]
    for load in loads:
        load.start()

    barrier = pltpu.get_barrier_semaphore()
    for k in order:
        pl.semaphore_signal(
            barrier, inc=1, device_id=peer(lax.rem(b + k, group)), device_id_type=MESH
        )
    for device in (to_a_next, to_a_prev):
        pl.semaphore_signal(barrier, inc=1, device_id=device, device_id_type=MESH)

    lane = lax.broadcasted_iota(jnp.int32, (TILE, LANES), 1)

    def column(tile, at):
        return jnp.broadcast_to(tile[:, at : at + 1], (TILE, LANES))

    loads[0].wait()
    lasts, firsts = [], []
    for t in range(tiles):
        last = jnp.zeros((TILE, LANES), jnp.float32)
        first = jnp.zeros((TILE, LANES), jnp.float32)
        for q in range(film):
            v = m[pl.ds(q * rows + t * TILE, TILE), :]
            chunk[pl.ds(t * TILE * film + q, TILE, stride=film), :] = v
            last = jnp.where(lane == q, column(v, LANES - 1), last)
            first = jnp.where(lane == film + q, column(v, 0), first)
        lasts.append(last)
        firsts.append(first)
    last = jnp.concatenate(lasts, axis=0)
    first = jnp.concatenate(firsts, axis=0)
    wide = lax.broadcasted_iota(jnp.int32, (rows, LANES), 1)
    deep = lax.broadcasted_iota(jnp.int32, (rows, LANES), 0)
    last = jnp.where(deep == 0, 0.0, pltpu.roll(last, 1, 0))
    first = jnp.where(deep == rows - 1, 0.0, pltpu.roll(first, rows - 1, 0))
    cols[...] = jnp.where(wide < film, last, first).reshape(rows, 1, LANES)

    def field(ref, comp, z):
        return ref[pl.ds((comp * nz + z) * rows, rows), :]

    def tile_of(ref, comp, z, t):
        return ref[pl.ds((comp * nz + z) * rows + t * TILE, TILE), :]

    def pack(ref, comps, at):
        packed = jnp.zeros((TILE, LANES), jnp.float32)
        for n, comp in enumerate(comps):
            for z in range(nz):
                for t in range(tiles):
                    v = tile_of(ref, comp, z, t)
                    packed = jnp.where(
                        lane == (n * nz + z) * tiles + t, column(v, at), packed
                    )
        return packed

    def unpack(packed, n, z):
        first = (n * nz + z) * tiles
        return jnp.concatenate([column(packed, first + t) for t in range(tiles)], axis=0)

    loads[1].wait()
    for n, comp in enumerate((1, 2)):
        hx_send[pl.ds(n * nz, nz), :] = h[
            pl.ds(comp * nz * rows + rows - 1, nz, stride=rows), :
        ]
    hy_send[...] = pack(h, (0, 2), LANES - 1)

    pl.semaphore_wait(barrier, group + 1)

    def send(src, dst, sem, device):
        copy = pltpu.make_async_remote_copy(
            src_ref=src,
            dst_ref=dst,
            send_sem=send_sem.at[0],
            recv_sem=sem,
            device_id=device,
            device_id_type=MESH,
        )
        copy.start()
        return copy

    def halo(src, dst, which, device):
        copy = pltpu.make_async_remote_copy(
            src_ref=src,
            dst_ref=dst,
            send_sem=halo_sem.at[0, which],
            recv_sem=halo_sem.at[1, which],
            device_id=device,
            device_id_type=MESH,
        )
        copy.start()
        return copy

    hx = halo(hx_send, hx_got, 0, to_a_next)
    hy = halo(hy_send, hy_got, 1, peer(b_next))
    mine = b // TILE
    own = [
        pltpu.make_async_copy(
            chunk.at[pl.ds(pl.multiple_of(b * film, film), film)],
            got.at[pl.ds(pl.multiple_of((b + 1) * film, film), film)],
            chunk_sem.at[mine],
        ),
        pltpu.make_async_copy(cols.at[b], got_cols.at[b], cols_sem.at[mine]),
    ]
    for copy in own:
        copy.start()
    for k in order:
        j = lax.rem(b + k, group)
        send(
            chunk.at[pl.ds(pl.multiple_of(j * film, film), film)],
            got.at[pl.ds(pl.multiple_of((b + 1) * film, film), film)],
            chunk_sem.at[mine],
            peer(j),
        )
        pltpu.make_async_remote_copy(
            src_ref=cols.at[j],
            dst_ref=got_cols.at[b],
            send_sem=send_sem.at[1],
            recv_sem=cols_sem.at[mine],
            device_id=peer(j),
            device_id_type=MESH,
        ).start()

    for load in loads[2:]:
        load.wait()
    index_x = a * rows + lax.broadcasted_iota(jnp.int32, (rows, LANES), 0)
    index_y = b * LANES + lax.broadcasted_iota(jnp.int32, (rows, LANES), 1)
    sigma = grade(index_x, count_x * rows) + grade(index_y, group * LANES)
    decay = (1.0 - sigma) / (1.0 + sigma)
    hstep = step_dt / (1.0 + sigma)
    film_step = step_dt / (film_eps * (1.0 + sigma))
    material = mat[...]
    eps = jnp.where(
        material == 0, 1.0, jnp.where(material == 1, 2.2, jnp.where(material == 2, 4.4, 9.8))
    ).astype(jnp.float32)
    upper_step = step_dt / (eps * (1.0 + sigma))

    hx.wait()
    hy.wait()
    left = jnp.where(b == 0, 0.0, hy_got[...])

    def below_x(v, n, z):
        edge = jnp.where(a == 0, 0.0, hx_got[pl.ds(n * nz + z, 1), :])
        return jnp.where(deep == 0, edge, pltpu.roll(v, 1, 0))

    def below_y(v, n, z):
        return jnp.where(wide == 0, unpack(left, n, z), pltpu.roll(v, 1, 1))

    under = None
    for z in range(nz):
        hx_z, hy_z, hz_z = (field(h, comp, z) for comp in range(3))
        back_zy = hz_z - below_y(hz_z, 1, z)
        back_zx = hz_z - below_x(hz_z, 1, z)
        back_yx = hy_z - below_x(hy_z, 0, z)
        back_xy = hx_z - below_y(hx_z, 0, z)
        back_yz = hy_z if under is None else hy_z - under[1]
        back_xz = hx_z if under is None else hx_z - under[0]
        comp_x = back_zy - back_yz
        if z == nz - 1:
            comp_x = comp_x - drv[...]
        comp_y = back_xz - back_zx
        comp_z = back_yx - back_xy
        estep = film_step if z < FZ else upper_step
        for comp, value in enumerate((comp_x, comp_y, comp_z)):
            e[pl.ds((comp * nz + z) * rows, rows), :] = decay * field(e, comp, z) + estep * value
        under = (hx_z, hy_z)

    for n, comp in enumerate((1, 2)):
        ex_send[pl.ds(n * nz, nz), :] = e[pl.ds(comp * nz * rows, nz, stride=rows), :]
    ey_send[...] = pack(e, (0, 2), 0)
    ex = halo(ex_send, ex_got, 2, to_a_prev)
    ey = halo(ey_send, ey_got, 3, peer(b_prev))

    ex.wait()
    ey.wait()
    right = jnp.where(b == group - 1, 0.0, ey_got[...])

    def above_x(v, n, z):
        edge = jnp.where(a == count_x - 1, 0.0, ex_got[pl.ds(n * nz + z, 1), :])
        return jnp.where(deep == rows - 1, edge, pltpu.roll(v, rows - 1, 0))

    def above_y(v, n, z):
        return jnp.where(wide == LANES - 1, unpack(right, n, z), pltpu.roll(v, LANES - 1, 1))

    for z in range(nz):
        ex_z, ey_z, ez_z = (field(e, comp, z) for comp in range(3))
        fore_zy = above_y(ez_z, 1, z) - ez_z
        fore_zx = above_x(ez_z, 1, z) - ez_z
        fore_yx = above_x(ey_z, 0, z) - ey_z
        fore_xy = above_y(ex_z, 0, z) - ex_z
        fore_yz = (field(e, 1, z + 1) if z < nz - 1 else 0.0) - ey_z
        fore_xz = (field(e, 0, z + 1) if z < nz - 1 else 0.0) - ex_z
        curls = (fore_zy - fore_yz, fore_xz - fore_zx, fore_yx - fore_xy)
        for comp, value in enumerate(curls):
            h[pl.ds((comp * nz + z) * rows, rows), :] = decay * field(h, comp, z) - hstep * value

    def rows_of(first, n):
        return got.at[pl.ds(first * film, n * film)]

    def wait_group(t):
        pltpu.make_async_copy(
            rows_of(1 + t * TILE, TILE), rows_of(1 + t * TILE, TILE), chunk_sem.at[t]
        ).wait()
        pltpu.make_async_copy(
            got_cols.at[pl.ds(t * TILE, TILE)], got_cols.at[pl.ds(t * TILE, TILE)], cols_sem.at[t]
        ).wait()

    def edge(src, dst, which, device):
        copy = pltpu.make_async_remote_copy(
            src_ref=rows_of(src, 1),
            dst_ref=rows_of(dst, 1),
            send_sem=edge_sem.at[0, which],
            recv_sem=edge_sem.at[1, which],
            device_id=device,
            device_id_type=MESH,
        )
        copy.start()
        return copy

    wait_group(0)
    low = edge(1, rows + 1, 0, to_a_prev)
    for t in range(1, tiles):
        wait_group(t)
    high = edge(rows, 0, 1, to_a_next)

    def spin(t):
        sides = got_cols[pl.ds(t * TILE, TILE)].reshape(TILE, LANES)

        def spins(comp, z, shift):
            first = (t * TILE + 1 + shift) * film + comp * FZ + z
            return got[pl.ds(first, TILE, stride=film), :]

        for z in range(FZ):
            centre = [spins(comp, z, 0) for comp in range(3)]
            heff = []
            for comp in range(3):
                v = centre[comp]
                q = comp * FZ + z
                y_up = jnp.where(
                    lane == LANES - 1, column(sides, film + q), pltpu.roll(v, LANES - 1, 1)
                )
                y_down = jnp.where(lane == 0, column(sides, q), pltpu.roll(v, 1, 1))
                lap = spins(comp, z, 1) + spins(comp, z, -1) + y_up + y_down
                if z < FZ - 1:
                    lap = lap + spins(comp, z + 1, 0)
                if z > 0:
                    lap = lap + spins(comp, z - 1, 0)
                lap = lap - 6.0 * v
                value = tile_of(h, comp, z, t) + exch_coef * lap
                if comp == 2:
                    value = value + 1.0 + 0.5 * v
                heff.append(value)
            mx, my, mz = centre
            tx = my * heff[2] - mz * heff[1]
            ty = mz * heff[0] - mx * heff[2]
            tz = mx * heff[1] - my * heff[0]
            dx = -gyro_coef * (tx + damp_coef * (my * tz - mz * ty))
            dy = -gyro_coef * (ty + damp_coef * (mz * tx - mx * tz))
            dz = -gyro_coef * (tz + damp_coef * (mx * ty - my * tx))
            for comp, d in enumerate((dx, dy, dz)):
                at = pl.ds((comp * nz + z) * rows + t * TILE, TILE)
                h[at, :] = h[at, :] - d
            big_x, big_y = largest(mx, my, mz)
            u = jnp.where(big_x, dy, jnp.where(big_y, dz, dx))
            v = jnp.where(big_x, dz, jnp.where(big_y, dx, dy))
            back[pl.ds(t * TILE * 2 * FZ + z, TILE, stride=2 * FZ), :] = u
            back[pl.ds(t * TILE * 2 * FZ + FZ + z, TILE, stride=2 * FZ), :] = v

    def part(ref, index):
        return ref.at[pl.ds(pl.multiple_of(index * 2 * FZ, 2 * FZ), 2 * FZ)]

    def send_back(t):
        for i in range(t * TILE, (t + 1) * TILE):

            @pl.when(b != i)
            def _():
                pltpu.make_async_remote_copy(
                    src_ref=part(back, i),
                    dst_ref=part(back_got, b),
                    send_sem=send_sem.at[2],
                    recv_sem=back_sem.at[mine],
                    device_id={"emx": a, "emy": i // grp, "grp": i % grp},
                    device_id_type=MESH,
                ).start()

            @pl.when(b == i)
            def _():
                pltpu.make_async_copy(part(back, i), part(back_got, b), back_sem.at[mine]).start()

    for t in range(1, tiles - 1):
        spin(t)
        send_back(t)

    low.wait()
    high.wait()

    @pl.when(a == 0)
    def _():
        got[pl.ds(0, film), :] = jnp.zeros((film, LANES), jnp.float32)

    @pl.when(a == count_x - 1)
    def _():
        got[pl.ds((rows + 1) * film, film), :] = jnp.zeros((film, LANES), jnp.float32)

    for t in sorted({0, tiles - 1}):
        spin(t)
        send_back(t)

    for t in range(tiles):
        landed = back_got.at[pl.ds(t * TILE * 2 * FZ, TILE * 2 * FZ)]
        pltpu.make_async_copy(landed, landed, back_sem.at[t]).wait()
        for z in range(FZ):
            places = [pl.ds((comp * FZ + z) * rows + t * TILE, TILE) for comp in range(3)]
            mx, my, mz = (m[at, :] for at in places)
            u = back_got[pl.ds(t * TILE * 2 * FZ + z, TILE, stride=2 * FZ), :]
            v = back_got[pl.ds(t * TILE * 2 * FZ + FZ + z, TILE, stride=2 * FZ), :]
            big_x, big_y = largest(mx, my, mz)
            big = jnp.where(big_x, mx, jnp.where(big_y, my, mz))
            mu = jnp.where(big_x, my, jnp.where(big_y, mz, mx))
            mv = jnp.where(big_x, mz, jnp.where(big_y, mx, my))
            tiny = jnp.abs(big) < 1e-30
            scale = jnp.where(tiny, 0.0, 1.0 / jnp.where(tiny, 1.0, big))
            w = -((mu * scale) * u + (mv * scale) * v)
            m[places[0], :] = mx + jnp.where(big_x, w, jnp.where(big_y, v, u))
            m[places[1], :] = my + jnp.where(big_x, u, jnp.where(big_y, w, v))
            m[places[2], :] = mz + jnp.where(big_x, v, jnp.where(big_y, u, w))

    for ref, sem in ((chunk, 0), (back, 2)):
        size = ref.shape[0] // group * (group - 1)
        sent = ref.at[pl.ds(0, size)]
        pltpu.make_async_copy(sent, sent, send_sem.at[sem]).wait()
    sent = cols.at[pl.ds(0, group - 1)]
    pltpu.make_async_copy(sent, sent, send_sem.at[1]).wait()


def store_kernel(e, h, m, e_out, h_out, m_out, sem):
    pairs = ((e, e_out), (h, h_out), (m, m_out))
    copies = [pltpu.make_async_copy(src, dst, sem.at[i]) for i, (src, dst) in enumerate(pairs)]
    for copy in copies:
        copy.start()
    for copy in copies:
        copy.wait()


def largest(mx, my, mz):
    sx, sy, sz = jnp.abs(mx), jnp.abs(my), jnp.abs(mz)
    big_x = (sx >= sy) & (sx >= sz)
    big_y = sy >= sz
    return big_x, big_y


def shards(efield, hfield, magnet, material, drive):
    _, nz, rows, cols_y = efield.shape
    count_x = lax.axis_size("emx")
    emy, grp = lax.axis_size("emy"), lax.axis_size("grp")
    group = emy * grp
    assert cols_y == LANES and rows == group and magnet.shape[2] == 1
    film = 3 * FZ
    tiles = rows // TILE
    assert 2 * nz * tiles <= LANES and 2 * film <= LANES
    f32 = jnp.float32
    field_shape = (3 * nz * rows, LANES)
    spin_shape = (film * group, LANES)
    dma = pltpu.SemaphoreType.DMA
    any_spec = pl.BlockSpec(memory_space=pl.ANY)
    sizes = (nz, rows, count_x, group, emy, grp)
    vmem_spec = pl.BlockSpec(memory_space=pltpu.VMEM)
    operands = [
        pltpu.with_memory_space_constraint(operand, pltpu.HBM)
        for operand in (
            efield.reshape(field_shape),
            hfield.reshape(field_shape),
            magnet.reshape(spin_shape),
            material,
            drive,
        )
    ]
    held = pl.pallas_call(
        functools.partial(step_kernel, sizes),
        out_shape=(
            pltpu.VMEM(field_shape, f32),
            pltpu.VMEM(field_shape, f32),
            pltpu.VMEM(spin_shape, f32),
        ),
        in_specs=[any_spec] * 5,
        out_specs=[vmem_spec] * 3,
        scratch_shapes=[
            pltpu.VMEM((rows, LANES), jnp.int32),
            pltpu.VMEM((rows, LANES), f32),
            pltpu.VMEM((group * film, LANES), f32),
            pltpu.VMEM((group, 1, LANES), f32),
            pltpu.VMEM(((rows + 2) * film, LANES), f32),
            pltpu.VMEM((rows, 1, LANES), f32),
            pltpu.VMEM((2 * nz, LANES), f32),
            pltpu.VMEM((2 * nz, LANES), f32),
            pltpu.VMEM((TILE, LANES), f32),
            pltpu.VMEM((TILE, LANES), f32),
            pltpu.VMEM((2 * nz, LANES), f32),
            pltpu.VMEM((2 * nz, LANES), f32),
            pltpu.VMEM((TILE, LANES), f32),
            pltpu.VMEM((TILE, LANES), f32),
            pltpu.VMEM((rows * 2 * FZ, LANES), f32),
            pltpu.VMEM((group * 2 * FZ, LANES), f32),
            dma((5,)),
            dma((3,)),
            dma((2, 4)),
            dma((tiles,)),
            dma((tiles,)),
            dma((2, 2)),
            dma((tiles,)),
        ],
        compiler_params=pltpu.CompilerParams(
            collective_id=0, has_side_effects=True, vmem_limit_bytes=32 * 1024 * 1024
        ),
    )(*operands)
    outs = pl.pallas_call(
        store_kernel,
        out_shape=(
            jax.ShapeDtypeStruct(field_shape, f32),
            jax.ShapeDtypeStruct(field_shape, f32),
            jax.ShapeDtypeStruct(spin_shape, f32),
        ),
        in_specs=[vmem_spec] * 3,
        out_specs=[any_spec] * 3,
        scratch_shapes=[dma((3,))],
    )(*(pltpu.with_memory_space_constraint(part, pltpu.VMEM) for part in held))
    return (
        outs[0].reshape(efield.shape),
        outs[1].reshape(hfield.shape),
        outs[2].reshape(magnet.shape),
    )


def solution(mesh):
    return jax.shard_map(
        shards,
        mesh=mesh,
        in_specs=(
            P(None, None, "emx", ("emy", "grp")),
            P(None, None, "emx", ("emy", "grp")),
            P(None, None, ("emx", "emy", "grp"), None),
            P("emx", ("emy", "grp")),
            P("emx", ("emy", "grp")),
        ),
        out_specs=(
            P(None, None, "emx", ("emy", "grp")),
            P(None, None, "emx", ("emy", "grp")),
            P(None, None, ("emx", "emy", "grp"), None),
        ),
        check_vma=False,
    )
```

```python
import functools

import jax
import jax.numpy as jnp
from jax import lax
from jax.experimental import pallas as pl
from jax.experimental.pallas import tpu as pltpu
from jax.sharding import PartitionSpec as P

FZ = 8
W = 8

step_dt = 0.5
film_eps = 15.0
exch_coef = 0.25
gyro_coef = 0.3
damp_coef = 0.1

MESH = pl.DeviceIdType.MESH
LANES = 128
CUT = 5
HALF = FZ // 2
PITCH = 16
TILE = 8


def grade(index, count):
    edge = jnp.minimum(index, count - 1 - index)
    depth = jnp.maximum(W - edge, 0).astype(jnp.float32) / W
    return 0.4 * depth * depth


def spread_order(count):
    half = count // 2
    order = [half]
    for step in range(1, half):
        order += [half + step, half - step]
    return order


def step_kernel(
    sizes,
    e_in, h_in, m_in, mat_in, drv_in,
    e, h, m,
    mat, drv,
    chunk_a, chunk_b, got_a, got_b,
    hx_send, hx_got, hy_send, hy_got,
    ex_send, ex_got, ey_send, ey_got,
    back, back_got,
    load_sem, send_sem, halo_sem, wave_sem, edge_sem, back_sem,
):
    nz, rows, count_x, group, emy, grp = sizes
    tiles = rows // TILE
    film = 3 * FZ
    a = lax.axis_index("emx")
    b = lax.axis_index("emy") * grp + lax.axis_index("grp")

    def peer(index):
        return {"emx": a, "emy": index // grp, "grp": lax.rem(index, grp)}

    a_next, a_prev = lax.rem(a + 1, count_x), lax.rem(a + count_x - 1, count_x)
    b_next, b_prev = lax.rem(b + 1, group), lax.rem(b + group - 1, group)
    to_a_next, to_a_prev = {"emx": a_next}, {"emx": a_prev}
    order = spread_order(group)

    def layers(ref, lo, hi, comp):
        first = (comp * FZ + lo) * rows
        return ref.at[pl.ds(first, (hi - lo) * rows)]

    m_loads = [
        [
            pltpu.make_async_copy(
                layers(m_in, lo, hi, comp), layers(m, lo, hi, comp), load_sem.at[4 + 3 * wave + comp]
            )
            for comp in range(3)
        ]
        for wave, (lo, hi) in enumerate(((0, CUT), (CUT, FZ)))
    ]
    loads = [
        pltpu.make_async_copy(src, dst, load_sem.at[i])
        for i, (src, dst) in enumerate(((h_in, h), (e_in, e), (mat_in, mat), (drv_in, drv)))
    ]
    for load in m_loads[0] + m_loads[1] + loads:
        load.start()

    barrier = pltpu.get_barrier_semaphore()
    for k in order:
        pl.semaphore_signal(
            barrier, inc=1, device_id=peer(lax.rem(b + k, group)), device_id_type=MESH
        )
    for device in (to_a_next, to_a_prev):
        pl.semaphore_signal(barrier, inc=1, device_id=device, device_id_type=MESH)

    lane = lax.broadcasted_iota(jnp.int32, (TILE, LANES), 1)
    wide = lax.broadcasted_iota(jnp.int32, (rows, LANES), 1)
    deep = lax.broadcasted_iota(jnp.int32, (rows, LANES), 0)

    def column(tile, at):
        return jnp.broadcast_to(tile[:, at : at + 1], (TILE, LANES))

    def wait_all(copies):
        for copy in copies:
            copy.wait()

    def place(z):
        return (chunk_a, z) if z < CUT else (chunk_b, z - CUT)

    def fill(lo, hi, lasts, firsts):
        for t in range(tiles):
            for comp in range(3):
                for z in range(lo, hi):
                    q = comp * FZ + z
                    v = m[pl.ds(q * rows + t * TILE, TILE), :]
                    ref, layer = place(z)
                    ref[pl.ds(t * TILE * PITCH + layer * 3 + comp, TILE, stride=PITCH), :] = v
                    lasts[t] = jnp.where(lane == q, column(v, LANES - 1), lasts[t])
                    firsts[t] = jnp.where(lane == film + q, column(v, 0), firsts[t])

    blank = jnp.zeros((TILE, LANES), jnp.float32)
    lasts, firsts = [blank] * tiles, [blank] * tiles
    wait_all(m_loads[0])
    fill(0, CUT, lasts, firsts)
    wait_all(m_loads[1])
    fill(CUT, FZ, lasts, firsts)
    last = jnp.concatenate(lasts, axis=0)
    first = jnp.concatenate(firsts, axis=0)
    last = jnp.where(deep == 0, 0.0, pltpu.roll(last, 1, 0))
    first = jnp.where(deep == rows - 1, 0.0, pltpu.roll(first, rows - 1, 0))
    edges = jnp.where(wide < film, last, first)
    for t in range(tiles):
        chunk_a[pl.ds(t * TILE * PITCH + 3 * CUT, TILE, stride=PITCH), :] = edges[
            t * TILE : (t + 1) * TILE
        ]

    def field(ref, comp, z):
        return ref[pl.ds((comp * nz + z) * rows, rows), :]

    def tile_of(ref, comp, z, t):
        return ref[pl.ds((comp * nz + z) * rows + t * TILE, TILE), :]

    def pack(ref, comps, at):
        packed = jnp.zeros((TILE, LANES), jnp.float32)
        for n, comp in enumerate(comps):
            for z in range(nz):
                for t in range(tiles):
                    v = tile_of(ref, comp, z, t)
                    packed = jnp.where(
                        lane == (n * nz + z) * tiles + t, column(v, at), packed
                    )
        return packed

    def unpack(packed, n, z):
        first = (n * nz + z) * tiles
        return jnp.concatenate([column(packed, first + t) for t in range(tiles)], axis=0)

    loads[0].wait()
    for n, comp in enumerate((1, 2)):
        hx_send[pl.ds(n * nz, nz), :] = h[
            pl.ds(comp * nz * rows + rows - 1, nz, stride=rows), :
        ]
    hy_send[...] = pack(h, (0, 2), LANES - 1)

    pl.semaphore_wait(barrier, group + 1)

    def halo(src, dst, which, device):
        copy = pltpu.make_async_remote_copy(
            src_ref=src,
            dst_ref=dst,
            send_sem=halo_sem.at[0, which],
            recv_sem=halo_sem.at[1, which],
            device_id=device,
            device_id_type=MESH,
        )
        copy.start()
        return copy

    def block(ref, index, size):
        return ref.at[pl.ds(pl.multiple_of(index * PITCH, PITCH), size)]

    hx = halo(hx_send, hx_got, 0, to_a_next)
    hy = halo(hy_send, hy_got, 1, peer(b_next))
    kind = (b + group - 2) // (group - 1) + b // (group - 1)
    waves = ((chunk_a, got_a, 3 * CUT + 1), (chunk_b, got_b, 3 * (FZ - CUT)))

    def send_wave(wave, part):
        src, dst, size = waves[wave]
        for k in part:
            j = lax.rem(b + k, group)
            pltpu.make_async_remote_copy(
                src_ref=block(src, j, size),
                dst_ref=block(dst, b + 1, size),
                send_sem=send_sem.at[wave],
                recv_sem=wave_sem.at[wave, kind],
                device_id=peer(j),
                device_id_type=MESH,
            ).start()

    for wave, (src, dst, size) in enumerate(waves):
        pltpu.make_async_copy(
            block(src, b, size), block(dst, b + 1, size), wave_sem.at[wave, kind]
        ).start()
    send_wave(0, order)

    for load in loads[1:]:
        load.wait()
    index_x = a * rows + deep
    index_y = b * LANES + wide
    sigma = grade(index_x, count_x * rows) + grade(index_y, group * LANES)
    decay = (1.0 - sigma) / (1.0 + sigma)
    hstep = step_dt / (1.0 + sigma)
    film_step = step_dt / (film_eps * (1.0 + sigma))
    material = mat[...]
    eps = jnp.where(
        material == 0, 1.0, jnp.where(material == 1, 2.2, jnp.where(material == 2, 4.4, 9.8))
    ).astype(jnp.float32)
    upper_step = step_dt / (eps * (1.0 + sigma))

    hx.wait()
    hy.wait()
    left = jnp.where(b == 0, 0.0, hy_got[...])

    def below_x(v, n, z):
        edge = jnp.where(a == 0, 0.0, hx_got[pl.ds(n * nz + z, 1), :])
        return jnp.where(deep == 0, edge, pltpu.roll(v, 1, 0))

    def below_y(v, n, z):
        return jnp.where(wide == 0, unpack(left, n, z), pltpu.roll(v, 1, 1))

    under = None
    for z in range(nz):
        hx_z, hy_z, hz_z = (field(h, comp, z) for comp in range(3))
        back_zy = hz_z - below_y(hz_z, 1, z)
        back_zx = hz_z - below_x(hz_z, 1, z)
        back_yx = hy_z - below_x(hy_z, 0, z)
        back_xy = hx_z - below_y(hx_z, 0, z)
        back_yz = hy_z if under is None else hy_z - under[1]
        back_xz = hx_z if under is None else hx_z - under[0]
        comp_x = back_zy - back_yz
        if z == nz - 1:
            comp_x = comp_x - drv[...]
        comp_y = back_xz - back_zx
        comp_z = back_yx - back_xy
        estep = film_step if z < FZ else upper_step
        for comp, value in enumerate((comp_x, comp_y, comp_z)):
            e[pl.ds((comp * nz + z) * rows, rows), :] = decay * field(e, comp, z) + estep * value
        under = (hx_z, hy_z)

    for n, comp in enumerate((1, 2)):
        ex_send[pl.ds(n * nz, nz), :] = e[pl.ds(comp * nz * rows, nz, stride=rows), :]
    ey_send[...] = pack(e, (0, 2), 0)
    ex = halo(ex_send, ex_got, 2, to_a_prev)
    ey = halo(ey_send, ey_got, 3, peer(b_prev))
    send_wave(1, order)

    def wait_wave(wave, which, count):
        _, dst, size = waves[wave]
        landed = dst.at[pl.ds(0, count * size)]
        pltpu.make_async_copy(landed, landed, wave_sem.at[wave, which]).wait()

    def edge(wave, src, dst, which, device):
        _, ref, size = waves[wave]
        copy = pltpu.make_async_remote_copy(
            src_ref=block(ref, src, size),
            dst_ref=block(ref, dst, size),
            send_sem=edge_sem.at[0, wave, which],
            recv_sem=edge_sem.at[1, wave, which],
            device_id=device,
            device_id_type=MESH,
        )
        copy.start()
        return copy

    def pass_on(wave):
        wait_wave(wave, 0, 1)
        low = edge(wave, 1, rows + 1, 0, to_a_prev)
        wait_wave(wave, 2, 1)
        high = edge(wave, rows, 0, 1, to_a_next)
        return low, high

    passed = [pass_on(0), None]

    ex.wait()
    ey.wait()
    right = jnp.where(b == group - 1, 0.0, ey_got[...])

    def above_x(v, n, z):
        edge = jnp.where(a == count_x - 1, 0.0, ex_got[pl.ds(n * nz + z, 1), :])
        return jnp.where(deep == rows - 1, edge, pltpu.roll(v, rows - 1, 0))

    def above_y(v, n, z):
        return jnp.where(wide == LANES - 1, unpack(right, n, z), pltpu.roll(v, LANES - 1, 1))

    for z in range(nz):
        ex_z, ey_z, ez_z = (field(e, comp, z) for comp in range(3))
        fore_zy = above_y(ez_z, 1, z) - ez_z
        fore_zx = above_x(ez_z, 1, z) - ez_z
        fore_yx = above_x(ey_z, 0, z) - ey_z
        fore_xy = above_y(ex_z, 0, z) - ex_z
        fore_yz = (field(e, 1, z + 1) if z < nz - 1 else 0.0) - ey_z
        fore_xz = (field(e, 0, z + 1) if z < nz - 1 else 0.0) - ex_z
        curls = (fore_zy - fore_yz, fore_xz - fore_zx, fore_yx - fore_xy)
        for comp, value in enumerate(curls):
            h[pl.ds((comp * nz + z) * rows, rows), :] = decay * field(h, comp, z) - hstep * value

    def spin(first, count, stride, half):
        def take(ref, base, pitch):
            return ref[pl.ds(base, count, stride=pitch), :]

        sides = take(got_a, (first + 1) * PITCH + 3 * CUT, stride * PITCH)
        lane = lax.broadcasted_iota(jnp.int32, (count, LANES), 1)

        def column(tile, at):
            return jnp.broadcast_to(tile[:, at : at + 1], (count, LANES))

        def spins(comp, z, shift):
            ref, layer = (got_a, z) if z < CUT else (got_b, z - CUT)
            return take(ref, (first + 1 + shift) * PITCH + layer * 3 + comp, stride * PITCH)

        for layer in range(HALF):
            z = half * HALF + layer
            centre = [spins(comp, z, 0) for comp in range(3)]
            heff = []
            for comp in range(3):
                v = centre[comp]
                q = comp * FZ + z
                y_up = jnp.where(
                    lane == LANES - 1, column(sides, film + q), pltpu.roll(v, LANES - 1, 1)
                )
                y_down = jnp.where(lane == 0, column(sides, q), pltpu.roll(v, 1, 1))
                lap = spins(comp, z, 1) + spins(comp, z, -1) + y_up + y_down
                if z < FZ - 1:
                    lap = lap + spins(comp, z + 1, 0)
                if z > 0:
                    lap = lap + spins(comp, z - 1, 0)
                lap = lap - 6.0 * v
                value = take(h, (comp * nz + z) * rows + first, stride) + exch_coef * lap
                if comp == 2:
                    value = value + 1.0 + 0.5 * v
                heff.append(value)
            mx, my, mz = centre
            tx = my * heff[2] - mz * heff[1]
            ty = mz * heff[0] - mx * heff[2]
            tz = mx * heff[1] - my * heff[0]
            dx = -gyro_coef * (tx + damp_coef * (my * tz - mz * ty))
            dy = -gyro_coef * (ty + damp_coef * (mz * tx - mx * tz))
            dz = -gyro_coef * (tz + damp_coef * (mx * ty - my * tx))
            for comp, d in enumerate((dx, dy, dz)):
                at = pl.ds((comp * nz + z) * rows + first, count, stride=stride)
                h[at, :] = h[at, :] - d
            big_x, big_y = largest(mx, my, mz)
            u = jnp.where(big_x, dy, jnp.where(big_y, dz, dx))
            v = jnp.where(big_x, dz, jnp.where(big_y, dx, dy))
            at = (half * rows + first) * 2 * HALF + 2 * layer
            back[pl.ds(at, count, stride=stride * 2 * HALF), :] = u
            back[pl.ds(at + 1, count, stride=stride * 2 * HALF), :] = v

    def part(ref, half, index):
        first = (half * group + index) * 2 * HALF
        return ref.at[pl.ds(pl.multiple_of(first, 2 * HALF), 2 * HALF)]

    def send_back(indices, half):
        for i in indices:

            @pl.when(b != i)
            def _():
                pltpu.make_async_remote_copy(
                    src_ref=part(back, half, i),
                    dst_ref=part(back_got, half, b),
                    send_sem=send_sem.at[2 + half],
                    recv_sem=back_sem.at[half],
                    device_id={"emx": a, "emy": i // grp, "grp": i % grp},
                    device_id_type=MESH,
                ).start()

            @pl.when(b == i)
            def _():
                pltpu.make_async_copy(
                    part(back, half, i), part(back_got, half, b), back_sem.at[half]
                ).start()

    def inner(half):
        wait_wave(half, 1, rows - 2)
        for first in range(1, rows - 1, TILE):
            count = min(TILE, rows - 1 - first)
            spin(first, count, 1, half)
            send_back(range(first, first + count), half)

    def outer(half):
        for copy in passed[half]:
            copy.wait()
        ref = waves[half][1]

        @pl.when(a == 0)
        def _():
            ref[pl.ds(0, PITCH), :] = jnp.zeros((PITCH, LANES), jnp.float32)

        @pl.when(a == count_x - 1)
        def _():
            ref[pl.ds((rows + 1) * PITCH, PITCH), :] = jnp.zeros((PITCH, LANES), jnp.float32)

        spin(0, 2, rows - 1, half)
        send_back((0, rows - 1), half)

    inner(0)
    passed[1] = pass_on(1)
    outer(0)
    inner(1)
    outer(1)

    for half in range(2):
        landed = back_got.at[pl.ds(half * group * 2 * HALF, group * 2 * HALF)]
        pltpu.make_async_copy(landed, landed, back_sem.at[half]).wait()
        for t in range(tiles):
            for layer in range(HALF):
                z = half * HALF + layer
                places = [pl.ds((comp * FZ + z) * rows + t * TILE, TILE) for comp in range(3)]
                mx, my, mz = (m[at, :] for at in places)
                at = (half * group + t * TILE) * 2 * HALF + 2 * layer
                u = back_got[pl.ds(at, TILE, stride=2 * HALF), :]
                v = back_got[pl.ds(at + 1, TILE, stride=2 * HALF), :]
                big_x, big_y = largest(mx, my, mz)
                big = jnp.where(big_x, mx, jnp.where(big_y, my, mz))
                mu = jnp.where(big_x, my, jnp.where(big_y, mz, mx))
                mv = jnp.where(big_x, mz, jnp.where(big_y, mx, my))
                tiny = jnp.abs(big) < 1e-30
                scale = jnp.where(tiny, 0.0, 1.0 / jnp.where(tiny, 1.0, big))
                w = -((mu * scale) * u + (mv * scale) * v)
                m[places[0], :] = mx + jnp.where(big_x, w, jnp.where(big_y, v, u))
                m[places[1], :] = my + jnp.where(big_x, u, jnp.where(big_y, w, v))
                m[places[2], :] = mz + jnp.where(big_x, v, jnp.where(big_y, u, w))

    for sem, size in enumerate((3 * CUT + 1, 3 * (FZ - CUT), 2 * HALF, 2 * HALF)):
        sent = chunk_a.at[pl.ds(0, (group - 1) * size)]
        pltpu.make_async_copy(sent, sent, send_sem.at[sem]).wait()


def store_kernel(e, h, m, e_out, h_out, m_out, sem):
    pairs = ((e, e_out), (h, h_out), (m, m_out))
    copies = [pltpu.make_async_copy(src, dst, sem.at[i]) for i, (src, dst) in enumerate(pairs)]
    for copy in copies:
        copy.start()
    for copy in copies:
        copy.wait()


def largest(mx, my, mz):
    sx, sy, sz = jnp.abs(mx), jnp.abs(my), jnp.abs(mz)
    big_x = (sx >= sy) & (sx >= sz)
    big_y = sy >= sz
    return big_x, big_y


def shards(efield, hfield, magnet, material, drive):
    _, nz, rows, cols_y = efield.shape
    count_x = lax.axis_size("emx")
    emy, grp = lax.axis_size("emy"), lax.axis_size("grp")
    group = emy * grp
    assert cols_y == LANES and rows == group and magnet.shape[2] == 1
    film = 3 * FZ
    tiles = rows // TILE
    assert 2 * nz * tiles <= LANES and 2 * film <= LANES
    f32 = jnp.float32
    field_shape = (3 * nz * rows, LANES)
    spin_shape = (film * group, LANES)
    dma = pltpu.SemaphoreType.DMA
    any_spec = pl.BlockSpec(memory_space=pl.ANY)
    sizes = (nz, rows, count_x, group, emy, grp)
    vmem_spec = pl.BlockSpec(memory_space=pltpu.VMEM)
    operands = [
        pltpu.with_memory_space_constraint(operand, pltpu.HBM)
        for operand in (
            efield.reshape(field_shape),
            hfield.reshape(field_shape),
            magnet.reshape(spin_shape),
            material,
            drive,
        )
    ]
    held = pl.pallas_call(
        functools.partial(step_kernel, sizes),
        out_shape=(
            pltpu.VMEM(field_shape, f32),
            pltpu.VMEM(field_shape, f32),
            pltpu.VMEM(spin_shape, f32),
        ),
        in_specs=[any_spec] * 5,
        out_specs=[vmem_spec] * 3,
        scratch_shapes=[
            pltpu.VMEM((rows, LANES), jnp.int32),
            pltpu.VMEM((rows, LANES), f32),
            pltpu.VMEM((group * PITCH, LANES), f32),
            pltpu.VMEM((group * PITCH, LANES), f32),
            pltpu.VMEM(((rows + 2) * PITCH, LANES), f32),
            pltpu.VMEM(((rows + 2) * PITCH, LANES), f32),
            pltpu.VMEM((2 * nz, LANES), f32),
            pltpu.VMEM((2 * nz, LANES), f32),
            pltpu.VMEM((TILE, LANES), f32),
            pltpu.VMEM((TILE, LANES), f32),
            pltpu.VMEM((2 * nz, LANES), f32),
            pltpu.VMEM((2 * nz, LANES), f32),
            pltpu.VMEM((TILE, LANES), f32),
            pltpu.VMEM((TILE, LANES), f32),
            pltpu.VMEM((rows * 2 * FZ, LANES), f32),
            pltpu.VMEM((group * 2 * FZ, LANES), f32),
            dma((10,)),
            dma((4,)),
            dma((2, 4)),
            dma((2, 3)),
            dma((2, 2, 2)),
            dma((2,)),
        ],
        compiler_params=pltpu.CompilerParams(
            collective_id=0, has_side_effects=True, vmem_limit_bytes=32 * 1024 * 1024
        ),
    )(*operands)
    outs = pl.pallas_call(
        store_kernel,
        out_shape=(
            jax.ShapeDtypeStruct(field_shape, f32),
            jax.ShapeDtypeStruct(field_shape, f32),
            jax.ShapeDtypeStruct(spin_shape, f32),
        ),
        in_specs=[vmem_spec] * 3,
        out_specs=[any_spec] * 3,
        scratch_shapes=[dma((3,))],
    )(*(pltpu.with_memory_space_constraint(part, pltpu.VMEM) for part in held))
    return (
        outs[0].reshape(efield.shape),
        outs[1].reshape(hfield.shape),
        outs[2].reshape(magnet.shape),
    )


def solution(mesh):
    return jax.shard_map(
        shards,
        mesh=mesh,
        in_specs=(
            P(None, None, "emx", ("emy", "grp")),
            P(None, None, "emx", ("emy", "grp")),
            P(None, None, ("emx", "emy", "grp"), None),
            P("emx", ("emy", "grp")),
            P("emx", ("emy", "grp")),
        ),
        out_specs=(
            P(None, None, "emx", ("emy", "grp")),
            P(None, None, "emx", ("emy", "grp")),
            P(None, None, ("emx", "emy", "grp"), None),
        ),
        check_vma=False,
    )
```

```python
import functools

import jax
import jax.numpy as jnp
from jax import lax
from jax.experimental import pallas as pl
from jax.experimental.pallas import tpu as pltpu
from jax.sharding import PartitionSpec as P

FZ = 8
W = 8

step_dt = 0.5
film_eps = 15.0
exch_coef = 0.25
gyro_coef = 0.3
damp_coef = 0.1

MESH = pl.DeviceIdType.MESH
LANES = 128
CUT = 5
HALF = FZ // 2
PITCH = 16
SEATS = 4
MIDDLE = 25
TILE = 8


def grade(index, count):
    edge = jnp.minimum(index, count - 1 - index)
    depth = jnp.maximum(W - edge, 0).astype(jnp.float32) / W
    return 0.4 * depth * depth


def far_first(count):
    return sorted(range(1, count), key=lambda step: -min(step, count - step))


def step_kernel(
    sizes,
    e_in, h_in, m_in, mat_in, drv_in,
    e, h, m,
    mat, drv,
    chunk_a, chunk_b, got_a, got_b,
    hx_send, hx_got, hy_send, hy_got,
    ex_send, ex_got, ey_send, ey_got,
    back, back_got,
    load_sem, ready_sem, send_sem, halo_sem, wave_sem, edge_sem, back_sem,
):
    nz, rows, count_x, group, emy, grp = sizes
    tiles = rows // TILE
    film = 3 * FZ
    a = lax.axis_index("emx")
    b = lax.axis_index("emy") * grp + lax.axis_index("grp")

    def peer(index):
        return {"emx": a, "emy": index // grp, "grp": lax.rem(index, grp)}

    a_next, a_prev = lax.rem(a + 1, count_x), lax.rem(a + count_x - 1, count_x)
    b_next, b_prev = lax.rem(b + 1, group), lax.rem(b + group - 1, group)
    to_a_next, to_a_prev = {"emx": a_next}, {"emx": a_prev}
    has_next, has_prev = a < count_x - 1, a > 0
    plane, seat = b // SEATS, lax.rem(b, SEATS)
    far = far_first(group // SEATS)
    same_seat = [(step, 0) for step in far]
    mates = [(0, turn) for turn in range(1, SEATS)]
    others = [(step, turn) for turn in range(1, SEATS) for step in far]

    def member(offset):
        step, turn = offset
        planes = group // SEATS
        return lax.rem(plane + step, planes) * SEATS + lax.rem(seat + turn, SEATS)

    def layers(ref, lo, hi, comp):
        first = (comp * FZ + lo) * rows
        return ref.at[pl.ds(first, (hi - lo) * rows)]

    m_loads = [
        [
            pltpu.make_async_copy(
                layers(m_in, lo, hi, comp), layers(m, lo, hi, comp), load_sem.at[4 + 3 * wave + comp]
            )
            for comp in range(3)
        ]
        for wave, (lo, hi) in enumerate(((0, CUT), (CUT, FZ)))
    ]
    loads = [
        pltpu.make_async_copy(src, dst, load_sem.at[i])
        for i, (src, dst) in enumerate(((h_in, h), (e_in, e), (mat_in, mat), (drv_in, drv)))
    ]
    for load in m_loads[0] + m_loads[1] + loads:
        load.start()

    barrier = pltpu.get_barrier_semaphore()

    def greet(device):
        pl.semaphore_signal(barrier, inc=1, device_id=device, device_id_type=MESH)

    for offset in same_seat + mates:
        greet(peer(member(offset)))

    @pl.when(has_next)
    def _():
        greet(to_a_next)

    @pl.when(has_prev)
    def _():
        greet(to_a_prev)

    lane = lax.broadcasted_iota(jnp.int32, (TILE, LANES), 1)
    wide = lax.broadcasted_iota(jnp.int32, (rows, LANES), 1)
    deep = lax.broadcasted_iota(jnp.int32, (rows, LANES), 0)

    def column(tile, at):
        return jnp.broadcast_to(tile[:, at : at + 1], (TILE, LANES))

    def wait_all(copies):
        for copy in copies:
            copy.wait()

    def place(z):
        return (chunk_a, z) if z < CUT else (chunk_b, z - CUT)

    def fill(lo, hi, lasts, firsts):
        for t in range(tiles):
            for comp in range(3):
                for z in range(lo, hi):
                    q = comp * FZ + z
                    v = m[pl.ds(q * rows + t * TILE, TILE), :]
                    ref, layer = place(z)
                    ref[pl.ds(t * TILE * PITCH + layer * 3 + comp, TILE, stride=PITCH), :] = v
                    lasts[t] = jnp.where(lane == q, column(v, LANES - 1), lasts[t])
                    firsts[t] = jnp.where(lane == film + q, column(v, 0), firsts[t])

    blank = jnp.zeros((TILE, LANES), jnp.float32)
    lasts, firsts = [blank] * tiles, [blank] * tiles
    wait_all(m_loads[0])
    fill(0, CUT, lasts, firsts)
    wait_all(m_loads[1])
    fill(CUT, FZ, lasts, firsts)
    last = jnp.concatenate(lasts, axis=0)
    first = jnp.concatenate(firsts, axis=0)
    last = jnp.where(deep == 0, 0.0, pltpu.roll(last, 1, 0))
    first = jnp.where(deep == rows - 1, 0.0, pltpu.roll(first, rows - 1, 0))
    edges = jnp.where(wide < film, last, first)
    for t in range(tiles):
        chunk_a[pl.ds(t * TILE * PITCH + 3 * CUT, TILE, stride=PITCH), :] = edges[
            t * TILE : (t + 1) * TILE
        ]

    def field(ref, comp, z):
        return ref[pl.ds((comp * nz + z) * rows, rows), :]

    def tile_of(ref, comp, z, t):
        return ref[pl.ds((comp * nz + z) * rows + t * TILE, TILE), :]

    def pack(ref, comps, at):
        packed = jnp.zeros((TILE, LANES), jnp.float32)
        for n, comp in enumerate(comps):
            for z in range(nz):
                for t in range(tiles):
                    v = tile_of(ref, comp, z, t)
                    packed = jnp.where(
                        lane == (n * nz + z) * tiles + t, column(v, at), packed
                    )
        return packed

    def unpack(packed, n, z):
        first = (n * nz + z) * tiles
        return jnp.concatenate([column(packed, first + t) for t in range(tiles)], axis=0)

    loads[0].wait()
    for n, comp in enumerate((1, 2)):
        hx_send[pl.ds(n * nz, nz), :] = h[
            pl.ds(comp * nz * rows + rows - 1, nz, stride=rows), :
        ]
    hy_send[...] = pack(h, (0, 2), LANES - 1)

    def halo(src, dst, which, device):
        return pltpu.make_async_remote_copy(
            src_ref=src,
            dst_ref=dst,
            send_sem=halo_sem.at[0, which],
            recv_sem=halo_sem.at[1, which],
            device_id=device,
            device_id_type=MESH,
        )

    def go(copy, sends):
        @pl.when(sends)
        def _():
            copy.start()

    def land(copy, sends, receives):
        @pl.when(receives)
        def _():
            copy.wait_recv()

        @pl.when(sends)
        def _():
            copy.wait_send()

    def block(ref, index, size):
        return ref.at[pl.ds(pl.multiple_of(index * PITCH, PITCH), size)]

    hx = halo(hx_send, hx_got, 0, to_a_next)
    hy = halo(hy_send, hy_got, 1, peer(b_next))
    kind = (b + group - 2) // (group - 1) + b // (group - 1)
    waves = ((chunk_a, got_a, 3 * CUT + 1), (chunk_b, got_b, 3 * (FZ - CUT)))

    def send_wave(wave, part):
        src, dst, size = waves[wave]
        for offset in part:
            j = member(offset)
            pltpu.make_async_remote_copy(
                src_ref=block(src, j, size),
                dst_ref=block(dst, b + 1, size),
                send_sem=send_sem.at[wave],
                recv_sem=wave_sem.at[wave, kind],
                device_id=peer(j),
                device_id_type=MESH,
            ).start()

    for wave, (src, dst, size) in enumerate(waves):
        pltpu.make_async_copy(
            block(src, b, size), block(dst, b + 1, size), wave_sem.at[wave, kind]
        ).start()
    pl.semaphore_wait(
        barrier, len(same_seat + mates) + jnp.int32(has_next) + jnp.int32(has_prev)
    )
    for offset in mates:
        pl.semaphore_signal(
            ready_sem, inc=1, device_id=peer(member(offset)), device_id_type=MESH
        )
    send_wave(0, same_seat)
    pl.semaphore_wait(ready_sem, len(mates))
    go(hx, has_next)
    hy.start()
    send_wave(0, others + mates)

    for load in loads[1:]:
        load.wait()
    index_x = a * rows + deep
    index_y = b * LANES + wide
    sigma = grade(index_x, count_x * rows) + grade(index_y, group * LANES)
    decay = (1.0 - sigma) / (1.0 + sigma)
    hstep = step_dt / (1.0 + sigma)
    film_step = step_dt / (film_eps * (1.0 + sigma))
    material = mat[...]
    eps = jnp.where(
        material == 0, 1.0, jnp.where(material == 1, 2.2, jnp.where(material == 2, 4.4, 9.8))
    ).astype(jnp.float32)
    upper_step = step_dt / (eps * (1.0 + sigma))

    land(hx, has_next, has_prev)
    hy.wait()
    left = jnp.where(b == 0, 0.0, hy_got[...])

    def below_x(v, n, z):
        edge = jnp.where(has_prev, hx_got[pl.ds(n * nz + z, 1), :], 0.0)
        return jnp.where(deep == 0, edge, pltpu.roll(v, 1, 0))

    def below_y(v, n, z):
        return jnp.where(wide == 0, unpack(left, n, z), pltpu.roll(v, 1, 1))

    under = None
    for z in range(nz):
        hx_z, hy_z, hz_z = (field(h, comp, z) for comp in range(3))
        back_zy = hz_z - below_y(hz_z, 1, z)
        back_zx = hz_z - below_x(hz_z, 1, z)
        back_yx = hy_z - below_x(hy_z, 0, z)
        back_xy = hx_z - below_y(hx_z, 0, z)
        back_yz = hy_z if under is None else hy_z - under[1]
        back_xz = hx_z if under is None else hx_z - under[0]
        comp_x = back_zy - back_yz
        if z == nz - 1:
            comp_x = comp_x - drv[...]
        comp_y = back_xz - back_zx
        comp_z = back_yx - back_xy
        estep = film_step if z < FZ else upper_step
        for comp, value in enumerate((comp_x, comp_y, comp_z)):
            e[pl.ds((comp * nz + z) * rows, rows), :] = decay * field(e, comp, z) + estep * value
        under = (hx_z, hy_z)

    for n, comp in enumerate((1, 2)):
        ex_send[pl.ds(n * nz, nz), :] = e[pl.ds(comp * nz * rows, nz, stride=rows), :]
    ey_send[...] = pack(e, (0, 2), 0)
    ex = halo(ex_send, ex_got, 2, to_a_prev)
    ey = halo(ey_send, ey_got, 3, peer(b_prev))
    go(ex, has_prev)
    ey.start()
    send_wave(1, same_seat + others + mates)

    def wait_wave(wave, which, count):
        _, dst, size = waves[wave]
        landed = dst.at[pl.ds(0, count * size)]
        pltpu.make_async_copy(landed, landed, wave_sem.at[wave, which]).wait()

    def edge(wave, src, dst, which, device):
        _, ref, size = waves[wave]
        return pltpu.make_async_remote_copy(
            src_ref=block(ref, src, size),
            dst_ref=block(ref, dst, size),
            send_sem=edge_sem.at[0, wave, which],
            recv_sem=edge_sem.at[1, wave, which],
            device_id=device,
            device_id_type=MESH,
        )

    def pass_on(wave):
        high = edge(wave, rows, 0, 1, to_a_next)
        low = edge(wave, 1, rows + 1, 0, to_a_prev)
        wait_wave(wave, 2, 1)
        go(high, has_next)
        wait_wave(wave, 0, 1)
        go(low, has_prev)
        return low, high

    passed = [pass_on(0), None]

    land(ex, has_prev, has_next)
    ey.wait()
    right = jnp.where(b == group - 1, 0.0, ey_got[...])

    def above_x(v, n, z):
        edge = jnp.where(has_next, ex_got[pl.ds(n * nz + z, 1), :], 0.0)
        return jnp.where(deep == rows - 1, edge, pltpu.roll(v, rows - 1, 0))

    def above_y(v, n, z):
        return jnp.where(wide == LANES - 1, unpack(right, n, z), pltpu.roll(v, LANES - 1, 1))

    for z in range(nz):
        ex_z, ey_z, ez_z = (field(e, comp, z) for comp in range(3))
        fore_zy = above_y(ez_z, 1, z) - ez_z
        fore_zx = above_x(ez_z, 1, z) - ez_z
        fore_yx = above_x(ey_z, 0, z) - ey_z
        fore_xy = above_y(ex_z, 0, z) - ex_z
        fore_yz = (field(e, 1, z + 1) if z < nz - 1 else 0.0) - ey_z
        fore_xz = (field(e, 0, z + 1) if z < nz - 1 else 0.0) - ex_z
        curls = (fore_zy - fore_yz, fore_xz - fore_zx, fore_yx - fore_xy)
        for comp, value in enumerate(curls):
            h[pl.ds((comp * nz + z) * rows, rows), :] = decay * field(h, comp, z) - hstep * value

    def spin(first, count, stride, half):
        def take(ref, base, pitch):
            return ref[pl.ds(base, count, stride=pitch), :]

        sides = take(got_a, (first + 1) * PITCH + 3 * CUT, stride * PITCH)
        lane = lax.broadcasted_iota(jnp.int32, (count, LANES), 1)

        def column(tile, at):
            return jnp.broadcast_to(tile[:, at : at + 1], (count, LANES))

        def spins(comp, z, shift):
            ref, layer = (got_a, z) if z < CUT else (got_b, z - CUT)
            return take(ref, (first + 1 + shift) * PITCH + layer * 3 + comp, stride * PITCH)

        for layer in range(HALF):
            z = half * HALF + layer
            centre = [spins(comp, z, 0) for comp in range(3)]
            heff = []
            for comp in range(3):
                v = centre[comp]
                q = comp * FZ + z
                y_up = jnp.where(
                    lane == LANES - 1, column(sides, film + q), pltpu.roll(v, LANES - 1, 1)
                )
                y_down = jnp.where(lane == 0, column(sides, q), pltpu.roll(v, 1, 1))
                lap = spins(comp, z, 1) + spins(comp, z, -1) + y_up + y_down
                if z < FZ - 1:
                    lap = lap + spins(comp, z + 1, 0)
                if z > 0:
                    lap = lap + spins(comp, z - 1, 0)
                lap = lap - 6.0 * v
                value = take(h, (comp * nz + z) * rows + first, stride) + exch_coef * lap
                if comp == 2:
                    value = value + 1.0 + 0.5 * v
                heff.append(value)
            mx, my, mz = centre
            tx = my * heff[2] - mz * heff[1]
            ty = mz * heff[0] - mx * heff[2]
            tz = mx * heff[1] - my * heff[0]
            dx = -gyro_coef * (tx + damp_coef * (my * tz - mz * ty))
            dy = -gyro_coef * (ty + damp_coef * (mz * tx - mx * tz))
            dz = -gyro_coef * (tz + damp_coef * (mx * ty - my * tx))
            for comp, d in enumerate((dx, dy, dz)):
                at = pl.ds((comp * nz + z) * rows + first, count, stride=stride)
                h[at, :] = h[at, :] - d
            big_x, big_y = largest(mx, my, mz)
            u = jnp.where(big_x, dy, jnp.where(big_y, dz, dx))
            v = jnp.where(big_x, dz, jnp.where(big_y, dx, dy))
            at = (half * rows + first) * 2 * HALF + 2 * layer
            back[pl.ds(at, count, stride=stride * 2 * HALF), :] = u
            back[pl.ds(at + 1, count, stride=stride * 2 * HALF), :] = v

    def part(ref, half, index):
        first = (half * group + index) * 2 * HALF
        return ref.at[pl.ds(pl.multiple_of(first, 2 * HALF), 2 * HALF)]

    def send_back(indices, half):
        for i in indices:

            @pl.when(b != i)
            def _():
                pltpu.make_async_remote_copy(
                    src_ref=part(back, half, i),
                    dst_ref=part(back_got, half, b),
                    send_sem=send_sem.at[2 + half],
                    recv_sem=back_sem.at[half],
                    device_id={"emx": a, "emy": i // grp, "grp": i % grp},
                    device_id_type=MESH,
                ).start()

            @pl.when(b == i)
            def _():
                pltpu.make_async_copy(
                    part(back, half, i), part(back_got, half, b), back_sem.at[half]
                ).start()

    def inner(half, lo, hi):
        for first in range(lo, hi, TILE):
            count = min(TILE, hi - first)
            spin(first, count, 1, half)
            send_back(range(first, first + count), half)

    def outer(half, row):
        low, high = passed[half]
        ref = waves[half][1]
        if row == 0:
            land(high, has_next, has_prev)
            known, ghost = has_prev, 0
        else:
            land(low, has_prev, has_next)
            known, ghost = has_next, rows + 1

        @pl.when(jnp.logical_not(known))
        def _():
            ref[pl.ds(ghost * PITCH, PITCH), :] = jnp.zeros((PITCH, LANES), jnp.float32)

        spin(row, 1, 1, half)
        send_back((row,), half)

    middle = min(MIDDLE, rows - 1)
    wait_wave(0, 1, rows - 2)
    inner(0, 1, middle)
    outer(0, 0)
    inner(0, middle, rows - 1)
    passed[1] = pass_on(1)
    outer(0, rows - 1)
    wait_wave(1, 1, rows - 2)
    inner(1, 1, middle)
    outer(1, 0)
    inner(1, middle, rows - 1)
    outer(1, rows - 1)

    for half in range(2):
        landed = back_got.at[pl.ds(half * group * 2 * HALF, group * 2 * HALF)]
        pltpu.make_async_copy(landed, landed, back_sem.at[half]).wait()
        for t in range(tiles):
            for layer in range(HALF):
                z = half * HALF + layer
                places = [pl.ds((comp * FZ + z) * rows + t * TILE, TILE) for comp in range(3)]
                mx, my, mz = (m[at, :] for at in places)
                at = (half * group + t * TILE) * 2 * HALF + 2 * layer
                u = back_got[pl.ds(at, TILE, stride=2 * HALF), :]
                v = back_got[pl.ds(at + 1, TILE, stride=2 * HALF), :]
                big_x, big_y = largest(mx, my, mz)
                big = jnp.where(big_x, mx, jnp.where(big_y, my, mz))
                mu = jnp.where(big_x, my, jnp.where(big_y, mz, mx))
                mv = jnp.where(big_x, mz, jnp.where(big_y, mx, my))
                tiny = jnp.abs(big) < 1e-30
                scale = jnp.where(tiny, 0.0, 1.0 / jnp.where(tiny, 1.0, big))
                w = -((mu * scale) * u + (mv * scale) * v)
                m[places[0], :] = mx + jnp.where(big_x, w, jnp.where(big_y, v, u))
                m[places[1], :] = my + jnp.where(big_x, u, jnp.where(big_y, w, v))
                m[places[2], :] = mz + jnp.where(big_x, v, jnp.where(big_y, u, w))

    for sem, size in enumerate((3 * CUT + 1, 3 * (FZ - CUT), 2 * HALF, 2 * HALF)):
        sent = chunk_a.at[pl.ds(0, (group - 1) * size)]
        pltpu.make_async_copy(sent, sent, send_sem.at[sem]).wait()


def store_kernel(e, h, m, e_out, h_out, m_out, sem):
    pairs = ((e, e_out), (h, h_out), (m, m_out))
    copies = [pltpu.make_async_copy(src, dst, sem.at[i]) for i, (src, dst) in enumerate(pairs)]
    for copy in copies:
        copy.start()
    for copy in copies:
        copy.wait()


def largest(mx, my, mz):
    sx, sy, sz = jnp.abs(mx), jnp.abs(my), jnp.abs(mz)
    big_x = (sx >= sy) & (sx >= sz)
    big_y = sy >= sz
    return big_x, big_y


def shards(efield, hfield, magnet, material, drive):
    _, nz, rows, cols_y = efield.shape
    count_x = lax.axis_size("emx")
    emy, grp = lax.axis_size("emy"), lax.axis_size("grp")
    group = emy * grp
    assert cols_y == LANES and rows == group and magnet.shape[2] == 1
    film = 3 * FZ
    tiles = rows // TILE
    assert 2 * nz * tiles <= LANES and 2 * film <= LANES
    f32 = jnp.float32
    field_shape = (3 * nz * rows, LANES)
    spin_shape = (film * group, LANES)
    dma = pltpu.SemaphoreType.DMA
    any_spec = pl.BlockSpec(memory_space=pl.ANY)
    sizes = (nz, rows, count_x, group, emy, grp)
    vmem_spec = pl.BlockSpec(memory_space=pltpu.VMEM)
    operands = [
        pltpu.with_memory_space_constraint(operand, pltpu.HBM)
        for operand in (
            efield.reshape(field_shape),
            hfield.reshape(field_shape),
            magnet.reshape(spin_shape),
            material,
            drive,
        )
    ]
    held = pl.pallas_call(
        functools.partial(step_kernel, sizes),
        out_shape=(
            pltpu.VMEM(field_shape, f32),
            pltpu.VMEM(field_shape, f32),
            pltpu.VMEM(spin_shape, f32),
        ),
        in_specs=[any_spec] * 5,
        out_specs=[vmem_spec] * 3,
        scratch_shapes=[
            pltpu.VMEM((rows, LANES), jnp.int32),
            pltpu.VMEM((rows, LANES), f32),
            pltpu.VMEM((group * PITCH, LANES), f32),
            pltpu.VMEM((group * PITCH, LANES), f32),
            pltpu.VMEM(((rows + 2) * PITCH, LANES), f32),
            pltpu.VMEM(((rows + 2) * PITCH, LANES), f32),
            pltpu.VMEM((2 * nz, LANES), f32),
            pltpu.VMEM((2 * nz, LANES), f32),
            pltpu.VMEM((TILE, LANES), f32),
            pltpu.VMEM((TILE, LANES), f32),
            pltpu.VMEM((2 * nz, LANES), f32),
            pltpu.VMEM((2 * nz, LANES), f32),
            pltpu.VMEM((TILE, LANES), f32),
            pltpu.VMEM((TILE, LANES), f32),
            pltpu.VMEM((rows * 2 * FZ, LANES), f32),
            pltpu.VMEM((group * 2 * FZ, LANES), f32),
            dma((10,)),
            pltpu.SemaphoreType.REGULAR,
            dma((4,)),
            dma((2, 4)),
            dma((2, 3)),
            dma((2, 2, 2)),
            dma((2,)),
        ],
        compiler_params=pltpu.CompilerParams(
            collective_id=0, has_side_effects=True, vmem_limit_bytes=32 * 1024 * 1024
        ),
    )(*operands)
    outs = pl.pallas_call(
        store_kernel,
        out_shape=(
            jax.ShapeDtypeStruct(field_shape, f32),
            jax.ShapeDtypeStruct(field_shape, f32),
            jax.ShapeDtypeStruct(spin_shape, f32),
        ),
        in_specs=[vmem_spec] * 3,
        out_specs=[any_spec] * 3,
        scratch_shapes=[dma((3,))],
    )(*(pltpu.with_memory_space_constraint(part, pltpu.VMEM) for part in held))
    return (
        outs[0].reshape(efield.shape),
        outs[1].reshape(hfield.shape),
        outs[2].reshape(magnet.shape),
    )


def solution(mesh):
    return jax.shard_map(
        shards,
        mesh=mesh,
        in_specs=(
            P(None, None, "emx", ("emy", "grp")),
            P(None, None, "emx", ("emy", "grp")),
            P(None, None, ("emx", "emy", "grp"), None),
            P("emx", ("emy", "grp")),
            P("emx", ("emy", "grp")),
        ),
        out_specs=(
            P(None, None, "emx", ("emy", "grp")),
            P(None, None, "emx", ("emy", "grp")),
            P(None, None, ("emx", "emy", "grp"), None),
        ),
        check_vma=False,
    )
```

```python
import functools

import jax
import jax.numpy as jnp
from jax import lax
from jax.experimental import pallas as pl
from jax.experimental.pallas import tpu as pltpu
from jax.sharding import PartitionSpec as P

FZ = 8
W = 8

step_dt = 0.5
film_eps = 15.0
exch_coef = 0.25
gyro_coef = 0.3
damp_coef = 0.1

MESH = pl.DeviceIdType.MESH
LANES = 128
CUT = 5
HALF = FZ // 2
PITCH = 16
SEATS = 4
CUTS = (9, 25, 9)
TILE = 8


def grade(index, count):
    edge = jnp.minimum(index, count - 1 - index)
    depth = jnp.maximum(W - edge, 0).astype(jnp.float32) / W
    return 0.4 * depth * depth


def far_first(count):
    return sorted(range(1, count), key=lambda step: -min(step, count - step))


def step_kernel(
    sizes,
    e_in, h_in, m_in, mat_in, drv_in,
    e, h, m, back_got,
    mat, drv,
    chunk_a, chunk_b, got_a, got_b,
    hx_send, hx_got, hy_send, hy_got,
    ex_send, ex_got, ey_send, ey_got,
    back,
    load_sem, ready_sem, send_sem, halo_sem, wave_sem, edge_sem, back_sem,
):
    nz, rows, count_x, group, emy, grp = sizes
    tiles = rows // TILE
    film = 3 * FZ
    a = lax.axis_index("emx")
    b = lax.axis_index("emy") * grp + lax.axis_index("grp")

    def peer(index):
        return {"emx": a, "emy": index // grp, "grp": lax.rem(index, grp)}

    a_next, a_prev = lax.rem(a + 1, count_x), lax.rem(a + count_x - 1, count_x)
    b_next, b_prev = lax.rem(b + 1, group), lax.rem(b + group - 1, group)
    to_a_next, to_a_prev = {"emx": a_next}, {"emx": a_prev}
    has_next, has_prev = a < count_x - 1, a > 0
    plane, seat = b // SEATS, lax.rem(b, SEATS)
    far = far_first(group // SEATS)
    same_seat = [(step, 0) for step in far]
    mates = [(0, turn) for turn in range(1, SEATS)]
    others = [(step, turn) for turn in range(1, SEATS) for step in far]

    def member(offset):
        step, turn = offset
        planes = group // SEATS
        return lax.rem(plane + step, planes) * SEATS + lax.rem(seat + turn, SEATS)

    def layers(ref, lo, hi, comp):
        first = (comp * FZ + lo) * rows
        return ref.at[pl.ds(first, (hi - lo) * rows)]

    m_loads = [
        [
            pltpu.make_async_copy(
                layers(m_in, lo, hi, comp), layers(m, lo, hi, comp), load_sem.at[4 + 3 * wave + comp]
            )
            for comp in range(3)
        ]
        for wave, (lo, hi) in enumerate(((0, CUT), (CUT, FZ)))
    ]
    loads = [
        pltpu.make_async_copy(src, dst, load_sem.at[i])
        for i, (src, dst) in enumerate(((h_in, h), (e_in, e), (mat_in, mat), (drv_in, drv)))
    ]
    for load in m_loads[0] + m_loads[1] + loads:
        load.start()

    barrier = pltpu.get_barrier_semaphore()

    def greet(device):
        pl.semaphore_signal(barrier, inc=1, device_id=device, device_id_type=MESH)

    for offset in same_seat + mates:
        greet(peer(member(offset)))

    @pl.when(has_next)
    def _():
        greet(to_a_next)

    @pl.when(has_prev)
    def _():
        greet(to_a_prev)

    lane = lax.broadcasted_iota(jnp.int32, (TILE, LANES), 1)
    wide = lax.broadcasted_iota(jnp.int32, (rows, LANES), 1)
    deep = lax.broadcasted_iota(jnp.int32, (rows, LANES), 0)

    def column(tile, at):
        return jnp.broadcast_to(tile[:, at : at + 1], (TILE, LANES))

    def wait_all(copies):
        for copy in copies:
            copy.wait()

    def place(z):
        return (chunk_a, z) if z < CUT else (chunk_b, z - CUT)

    def fill(lo, hi, lasts, firsts):
        for t in range(tiles):
            for comp in range(3):
                for z in range(lo, hi):
                    q = comp * FZ + z
                    v = m[pl.ds(q * rows + t * TILE, TILE), :]
                    ref, layer = place(z)
                    ref[pl.ds(t * TILE * PITCH + layer * 3 + comp, TILE, stride=PITCH), :] = v
                    lasts[t] = jnp.where(lane == q, column(v, LANES - 1), lasts[t])
                    firsts[t] = jnp.where(lane == film + q, column(v, 0), firsts[t])

    blank = jnp.zeros((TILE, LANES), jnp.float32)
    lasts, firsts = [blank] * tiles, [blank] * tiles
    wait_all(m_loads[0])
    fill(0, CUT, lasts, firsts)
    wait_all(m_loads[1])
    fill(CUT, FZ, lasts, firsts)
    last = jnp.concatenate(lasts, axis=0)
    first = jnp.concatenate(firsts, axis=0)
    last = jnp.where(deep == 0, 0.0, pltpu.roll(last, 1, 0))
    first = jnp.where(deep == rows - 1, 0.0, pltpu.roll(first, rows - 1, 0))
    edges = jnp.where(wide < film, last, first)
    for t in range(tiles):
        chunk_a[pl.ds(t * TILE * PITCH + 3 * CUT, TILE, stride=PITCH), :] = edges[
            t * TILE : (t + 1) * TILE
        ]

    def field(ref, comp, z):
        return ref[pl.ds((comp * nz + z) * rows, rows), :]

    def tile_of(ref, comp, z, t):
        return ref[pl.ds((comp * nz + z) * rows + t * TILE, TILE), :]

    def pack(ref, comps, at):
        packed = jnp.zeros((TILE, LANES), jnp.float32)
        for n, comp in enumerate(comps):
            for z in range(nz):
                for t in range(tiles):
                    v = tile_of(ref, comp, z, t)
                    packed = jnp.where(
                        lane == (n * nz + z) * tiles + t, column(v, at), packed
                    )
        return packed

    def unpack(packed, n, z):
        first = (n * nz + z) * tiles
        return jnp.concatenate([column(packed, first + t) for t in range(tiles)], axis=0)

    loads[0].wait()
    for n, comp in enumerate((1, 2)):
        hx_send[pl.ds(n * nz, nz), :] = h[
            pl.ds(comp * nz * rows + rows - 1, nz, stride=rows), :
        ]
    hy_send[...] = pack(h, (0, 2), LANES - 1)

    def halo(src, dst, which, device):
        return pltpu.make_async_remote_copy(
            src_ref=src,
            dst_ref=dst,
            send_sem=halo_sem.at[0, which],
            recv_sem=halo_sem.at[1, which],
            device_id=device,
            device_id_type=MESH,
        )

    def go(copy, sends):
        @pl.when(sends)
        def _():
            copy.start()

    def land(copy, sends, receives):
        @pl.when(receives)
        def _():
            copy.wait_recv()

        @pl.when(sends)
        def _():
            copy.wait_send()

    def block(ref, index, size):
        return ref.at[pl.ds(pl.multiple_of(index * PITCH, PITCH), size)]

    hx = halo(hx_send, hx_got, 0, to_a_next)
    hy = halo(hy_send, hy_got, 1, peer(b_next))
    kind = (b + group - 2) // (group - 1) + b // (group - 1)
    waves = ((chunk_a, got_a, 3 * CUT + 1), (chunk_b, got_b, 3 * (FZ - CUT)))

    def send_wave(wave, part):
        src, dst, size = waves[wave]
        for offset in part:
            j = member(offset)
            pltpu.make_async_remote_copy(
                src_ref=block(src, j, size),
                dst_ref=block(dst, b + 1, size),
                send_sem=send_sem.at[wave],
                recv_sem=wave_sem.at[wave, kind],
                device_id=peer(j),
                device_id_type=MESH,
            ).start()

    for wave, (src, dst, size) in enumerate(waves):
        pltpu.make_async_copy(
            block(src, b, size), block(dst, b + 1, size), wave_sem.at[wave, kind]
        ).start()
    pl.semaphore_wait(
        barrier, len(same_seat + mates) + jnp.int32(has_next) + jnp.int32(has_prev)
    )
    for offset in mates:
        pl.semaphore_signal(
            ready_sem, inc=1, device_id=peer(member(offset)), device_id_type=MESH
        )
    send_wave(0, same_seat)
    pl.semaphore_wait(ready_sem, len(mates))
    go(hx, has_next)
    hy.start()
    send_wave(0, others + mates)

    @pl.when(b == rows - 1)
    def _():
        send_wave(1, same_seat + others + mates)


    for load in loads[1:]:
        load.wait()
    index_x = a * rows + deep
    index_y = b * LANES + wide
    sigma = grade(index_x, count_x * rows) + grade(index_y, group * LANES)
    decay = (1.0 - sigma) / (1.0 + sigma)
    hstep = step_dt / (1.0 + sigma)
    film_step = step_dt / (film_eps * (1.0 + sigma))
    material = mat[...]
    eps = jnp.where(
        material == 0, 1.0, jnp.where(material == 1, 2.2, jnp.where(material == 2, 4.4, 9.8))
    ).astype(jnp.float32)
    upper_step = step_dt / (eps * (1.0 + sigma))

    land(hx, has_next, has_prev)
    hy.wait()
    left = jnp.where(b == 0, 0.0, hy_got[...])

    def below_x(v, n, z):
        edge = jnp.where(has_prev, hx_got[pl.ds(n * nz + z, 1), :], 0.0)
        return jnp.where(deep == 0, edge, pltpu.roll(v, 1, 0))

    def below_y(v, n, z):
        return jnp.where(wide == 0, unpack(left, n, z), pltpu.roll(v, 1, 1))

    under = None
    for z in range(nz):
        hx_z, hy_z, hz_z = (field(h, comp, z) for comp in range(3))
        back_zy = hz_z - below_y(hz_z, 1, z)
        back_zx = hz_z - below_x(hz_z, 1, z)
        back_yx = hy_z - below_x(hy_z, 0, z)
        back_xy = hx_z - below_y(hx_z, 0, z)
        back_yz = hy_z if under is None else hy_z - under[1]
        back_xz = hx_z if under is None else hx_z - under[0]
        comp_x = back_zy - back_yz
        if z == nz - 1:
            comp_x = comp_x - drv[...]
        comp_y = back_xz - back_zx
        comp_z = back_yx - back_xy
        estep = film_step if z < FZ else upper_step
        for comp, value in enumerate((comp_x, comp_y, comp_z)):
            e[pl.ds((comp * nz + z) * rows, rows), :] = decay * field(e, comp, z) + estep * value
        under = (hx_z, hy_z)

    for n, comp in enumerate((1, 2)):
        ex_send[pl.ds(n * nz, nz), :] = e[pl.ds(comp * nz * rows, nz, stride=rows), :]
    ey_send[...] = pack(e, (0, 2), 0)
    ex = halo(ex_send, ex_got, 2, to_a_prev)
    ey = halo(ey_send, ey_got, 3, peer(b_prev))
    go(ex, has_prev)
    ey.start()

    @pl.when(b != rows - 1)
    def _():
        send_wave(1, same_seat + others + mates)

    def wait_wave(wave, which, count):
        _, dst, size = waves[wave]
        landed = dst.at[pl.ds(0, count * size)]
        pltpu.make_async_copy(landed, landed, wave_sem.at[wave, which]).wait()

    def edge(wave, src, dst, which, device):
        _, ref, size = waves[wave]
        return pltpu.make_async_remote_copy(
            src_ref=block(ref, src, size),
            dst_ref=block(ref, dst, size),
            send_sem=edge_sem.at[0, wave, which],
            recv_sem=edge_sem.at[1, wave, which],
            device_id=device,
            device_id_type=MESH,
        )

    high = [edge(wave, rows, 0, 1, to_a_next) for wave in range(2)]
    low = [edge(wave, 1, rows + 1, 0, to_a_prev) for wave in range(2)]

    def pass_high(wave):
        wait_wave(wave, 2, 1)
        go(high[wave], has_next)

    def pass_low(wave):
        wait_wave(wave, 0, 1)
        go(low[wave], has_prev)

    pass_high(0)
    pass_low(0)

    land(ex, has_prev, has_next)
    ey.wait()
    right = jnp.where(b == group - 1, 0.0, ey_got[...])

    def above_x(v, n, z):
        edge = jnp.where(has_next, ex_got[pl.ds(n * nz + z, 1), :], 0.0)
        return jnp.where(deep == rows - 1, edge, pltpu.roll(v, rows - 1, 0))

    def above_y(v, n, z):
        return jnp.where(wide == LANES - 1, unpack(right, n, z), pltpu.roll(v, LANES - 1, 1))

    for z in range(nz):
        ex_z, ey_z, ez_z = (field(e, comp, z) for comp in range(3))
        fore_zy = above_y(ez_z, 1, z) - ez_z
        fore_zx = above_x(ez_z, 1, z) - ez_z
        fore_yx = above_x(ey_z, 0, z) - ey_z
        fore_xy = above_y(ex_z, 0, z) - ex_z
        fore_yz = (field(e, 1, z + 1) if z < nz - 1 else 0.0) - ey_z
        fore_xz = (field(e, 0, z + 1) if z < nz - 1 else 0.0) - ex_z
        curls = (fore_zy - fore_yz, fore_xz - fore_zx, fore_yx - fore_xy)
        for comp, value in enumerate(curls):
            h[pl.ds((comp * nz + z) * rows, rows), :] = decay * field(h, comp, z) - hstep * value

    def spin(first, count, stride, half):
        def take(ref, base, pitch):
            return ref[pl.ds(base, count, stride=pitch), :]

        sides = take(got_a, (first + 1) * PITCH + 3 * CUT, stride * PITCH)
        lane = lax.broadcasted_iota(jnp.int32, (count, LANES), 1)

        def column(tile, at):
            return jnp.broadcast_to(tile[:, at : at + 1], (count, LANES))

        def spins(comp, z, shift):
            ref, layer = (got_a, z) if z < CUT else (got_b, z - CUT)
            return take(ref, (first + 1 + shift) * PITCH + layer * 3 + comp, stride * PITCH)

        for layer in range(HALF):
            z = half * HALF + layer
            centre = [spins(comp, z, 0) for comp in range(3)]
            heff = []
            for comp in range(3):
                v = centre[comp]
                q = comp * FZ + z
                y_up = jnp.where(
                    lane == LANES - 1, column(sides, film + q), pltpu.roll(v, LANES - 1, 1)
                )
                y_down = jnp.where(lane == 0, column(sides, q), pltpu.roll(v, 1, 1))
                lap = spins(comp, z, 1) + spins(comp, z, -1) + y_up + y_down
                if z < FZ - 1:
                    lap = lap + spins(comp, z + 1, 0)
                if z > 0:
                    lap = lap + spins(comp, z - 1, 0)
                lap = lap - 6.0 * v
                value = take(h, (comp * nz + z) * rows + first, stride) + exch_coef * lap
                if comp == 2:
                    value = value + 1.0 + 0.5 * v
                heff.append(value)
            mx, my, mz = centre
            tx = my * heff[2] - mz * heff[1]
            ty = mz * heff[0] - mx * heff[2]
            tz = mx * heff[1] - my * heff[0]
            dx = -gyro_coef * (tx + damp_coef * (my * tz - mz * ty))
            dy = -gyro_coef * (ty + damp_coef * (mz * tx - mx * tz))
            dz = -gyro_coef * (tz + damp_coef * (mx * ty - my * tx))
            for comp, d in enumerate((dx, dy, dz)):
                at = pl.ds((comp * nz + z) * rows + first, count, stride=stride)
                h[at, :] = h[at, :] - d
            big_x, big_y = largest(mx, my, mz)
            u = jnp.where(big_x, dy, jnp.where(big_y, dz, dx))
            v = jnp.where(big_x, dz, jnp.where(big_y, dx, dy))
            at = (half * rows + first) * 2 * HALF + 2 * layer
            back[pl.ds(at, count, stride=stride * 2 * HALF), :] = u
            back[pl.ds(at + 1, count, stride=stride * 2 * HALF), :] = v

    def part(ref, half, index):
        first = (half * group + index) * 2 * HALF
        return ref.at[pl.ds(pl.multiple_of(first, 2 * HALF), 2 * HALF)]

    def send_back(indices, half):
        for i in indices:

            @pl.when(b != i)
            def _():
                pltpu.make_async_remote_copy(
                    src_ref=part(back, half, i),
                    dst_ref=part(back_got, half, b),
                    send_sem=send_sem.at[2 + half],
                    recv_sem=back_sem.at[half],
                    device_id={"emx": a, "emy": i // grp, "grp": i % grp},
                    device_id_type=MESH,
                ).start()

            @pl.when(b == i)
            def _():
                pltpu.make_async_copy(
                    part(back, half, i), part(back_got, half, b), back_sem.at[half]
                ).start()

    def inner(half, lo, hi):
        for first in range(lo, hi, TILE):
            count = min(TILE, hi - first)
            spin(first, count, 1, half)
            send_back(range(first, first + count), half)

    def outer(half, row):
        ref = waves[half][1]
        if row == 0:
            land(high[half], has_next, has_prev)
            known, ghost = has_prev, 0
        else:
            land(low[half], has_prev, has_next)
            known, ghost = has_next, rows + 1

        @pl.when(jnp.logical_not(known))
        def _():
            ref[pl.ds(ghost * PITCH, PITCH), :] = jnp.zeros((PITCH, LANES), jnp.float32)

        spin(row, 1, 1, half)
        send_back((row,), half)

    cuts = [min(cut, rows - 1) for cut in CUTS]
    wait_wave(0, 1, rows - 2)
    inner(0, 1, cuts[0])
    pass_high(1)
    inner(0, cuts[0], cuts[1])
    outer(0, 0)
    inner(0, cuts[1], rows - 1)
    pass_low(1)
    outer(0, rows - 1)
    wait_wave(1, 1, rows - 2)
    inner(1, 1, cuts[2])
    outer(1, 0)
    inner(1, cuts[2], rows - 1)
    outer(1, rows - 1)

    for half in range(2):
        landed = back_got.at[pl.ds(half * group * 2 * HALF, group * 2 * HALF)]
        pltpu.make_async_copy(landed, landed, back_sem.at[half]).wait()
        if half == 0:
            turn_magnet(m, back_got, group, half)

    for sem, size in enumerate((3 * CUT + 1, 3 * (FZ - CUT), 2 * HALF, 2 * HALF)):
        sent = chunk_a.at[pl.ds(0, (group - 1) * size)]
        pltpu.make_async_copy(sent, sent, send_sem.at[sem]).wait()


def turn_magnet(m, back_got, rows, half):
    for t in range(rows // TILE):
        for layer in range(HALF):
            z = half * HALF + layer
            places = [pl.ds((comp * FZ + z) * rows + t * TILE, TILE) for comp in range(3)]
            mx, my, mz = (m[at, :] for at in places)
            at = (half * rows + t * TILE) * 2 * HALF + 2 * layer
            u = back_got[pl.ds(at, TILE, stride=2 * HALF), :]
            v = back_got[pl.ds(at + 1, TILE, stride=2 * HALF), :]
            big_x, big_y = largest(mx, my, mz)
            big = jnp.where(big_x, mx, jnp.where(big_y, my, mz))
            mu = jnp.where(big_x, my, jnp.where(big_y, mz, mx))
            mv = jnp.where(big_x, mz, jnp.where(big_y, mx, my))
            tiny = jnp.abs(big) < 1e-30
            scale = jnp.where(tiny, 0.0, 1.0 / jnp.where(tiny, 1.0, big))
            w = -((mu * scale) * u + (mv * scale) * v)
            m[places[0], :] = mx + jnp.where(big_x, w, jnp.where(big_y, v, u))
            m[places[1], :] = my + jnp.where(big_x, u, jnp.where(big_y, w, v))
            m[places[2], :] = mz + jnp.where(big_x, v, jnp.where(big_y, u, w))


def store_kernel(rows, e, h, m, back_got, e_out, h_out, m_out, part, sem):
    size = HALF * rows
    copies = [
        pltpu.make_async_copy(src, dst, sem.at[i]) for i, (src, dst) in enumerate(((e, e_out), (h, h_out)))
    ]
    for comp in range(3):
        at = pl.ds(comp * FZ * rows, size)
        copies.append(pltpu.make_async_copy(m.at[at], m_out.at[at], sem.at[2 + comp]))
    for copy in copies:
        copy.start()
    for comp in range(3):
        part[pl.ds((comp * FZ + HALF) * rows, size), :] = m[pl.ds((comp * FZ + HALF) * rows, size), :]
    turn_magnet(part, back_got, rows, 1)
    for comp in range(3):
        at = pl.ds((comp * FZ + HALF) * rows, size)
        copy = pltpu.make_async_copy(part.at[at], m_out.at[at], sem.at[5 + comp])
        copy.start()
        copies.append(copy)
    for copy in copies:
        copy.wait()


def largest(mx, my, mz):
    sx, sy, sz = jnp.abs(mx), jnp.abs(my), jnp.abs(mz)
    big_x = (sx >= sy) & (sx >= sz)
    big_y = sy >= sz
    return big_x, big_y


def shards(efield, hfield, magnet, material, drive):
    _, nz, rows, cols_y = efield.shape
    count_x = lax.axis_size("emx")
    emy, grp = lax.axis_size("emy"), lax.axis_size("grp")
    group = emy * grp
    assert cols_y == LANES and rows == group and magnet.shape[2] == 1
    film = 3 * FZ
    tiles = rows // TILE
    assert 2 * nz * tiles <= LANES and 2 * film <= LANES
    f32 = jnp.float32
    field_shape = (3 * nz * rows, LANES)
    spin_shape = (film * group, LANES)
    dma = pltpu.SemaphoreType.DMA
    any_spec = pl.BlockSpec(memory_space=pl.ANY)
    sizes = (nz, rows, count_x, group, emy, grp)
    vmem_spec = pl.BlockSpec(memory_space=pltpu.VMEM)
    operands = [
        pltpu.with_memory_space_constraint(operand, pltpu.HBM)
        for operand in (
            efield.reshape(field_shape),
            hfield.reshape(field_shape),
            magnet.reshape(spin_shape),
            material,
            drive,
        )
    ]
    held = pl.pallas_call(
        functools.partial(step_kernel, sizes),
        out_shape=(
            pltpu.VMEM(field_shape, f32),
            pltpu.VMEM(field_shape, f32),
            pltpu.VMEM(spin_shape, f32),
            pltpu.VMEM((group * 2 * FZ, LANES), f32),
        ),
        in_specs=[any_spec] * 5,
        out_specs=[vmem_spec] * 4,
        scratch_shapes=[
            pltpu.VMEM((rows, LANES), jnp.int32),
            pltpu.VMEM((rows, LANES), f32),
            pltpu.VMEM((group * PITCH, LANES), f32),
            pltpu.VMEM((group * PITCH, LANES), f32),
            pltpu.VMEM(((rows + 2) * PITCH, LANES), f32),
            pltpu.VMEM(((rows + 2) * PITCH, LANES), f32),
            pltpu.VMEM((2 * nz, LANES), f32),
            pltpu.VMEM((2 * nz, LANES), f32),
            pltpu.VMEM((TILE, LANES), f32),
            pltpu.VMEM((TILE, LANES), f32),
            pltpu.VMEM((2 * nz, LANES), f32),
            pltpu.VMEM((2 * nz, LANES), f32),
            pltpu.VMEM((TILE, LANES), f32),
            pltpu.VMEM((TILE, LANES), f32),
            pltpu.VMEM((rows * 2 * FZ, LANES), f32),
            dma((10,)),
            pltpu.SemaphoreType.REGULAR,
            dma((4,)),
            dma((2, 4)),
            dma((2, 3)),
            dma((2, 2, 2)),
            dma((2,)),
        ],
        compiler_params=pltpu.CompilerParams(
            collective_id=0, has_side_effects=True, vmem_limit_bytes=32 * 1024 * 1024
        ),
    )(*operands)
    outs = pl.pallas_call(
        functools.partial(store_kernel, rows),
        out_shape=(
            jax.ShapeDtypeStruct(field_shape, f32),
            jax.ShapeDtypeStruct(field_shape, f32),
            jax.ShapeDtypeStruct(spin_shape, f32),
        ),
        in_specs=[vmem_spec] * 4,
        out_specs=[any_spec] * 3,
        scratch_shapes=[pltpu.VMEM(spin_shape, f32), dma((8,))],
    )(*(pltpu.with_memory_space_constraint(part, pltpu.VMEM) for part in held))
    return (
        outs[0].reshape(efield.shape),
        outs[1].reshape(hfield.shape),
        outs[2].reshape(magnet.shape),
    )


def solution(mesh):
    return jax.shard_map(
        shards,
        mesh=mesh,
        in_specs=(
            P(None, None, "emx", ("emy", "grp")),
            P(None, None, "emx", ("emy", "grp")),
            P(None, None, ("emx", "emy", "grp"), None),
            P("emx", ("emy", "grp")),
            P("emx", ("emy", "grp")),
        ),
        out_specs=(
            P(None, None, "emx", ("emy", "grp")),
            P(None, None, "emx", ("emy", "grp")),
            P(None, None, ("emx", "emy", "grp"), None),
        ),
        check_vma=False,
    )
```

```python
import functools

import jax
import jax.numpy as jnp
from jax import lax
from jax.experimental import pallas as pl
from jax.experimental.pallas import tpu as pltpu
from jax.sharding import PartitionSpec as P

FZ = 8
W = 8

step_dt = 0.5
film_eps = 15.0
exch_coef = 0.25
gyro_coef = 0.3
damp_coef = 0.1

MESH = pl.DeviceIdType.MESH
LANES = 128
CUT = 5
HALF = FZ // 2
PITCH = 16
SEATS = 4
CUTS = (9, 25, 9)
TILE = 8


def grade(index, count):
    edge = jnp.minimum(index, count - 1 - index)
    depth = jnp.maximum(W - edge, 0).astype(jnp.float32) / W
    return 0.4 * depth * depth


def far_first(count):
    return sorted(range(1, count), key=lambda step: -min(step, count - step))


def step_kernel(
    sizes,
    e_in, h_in, m_in, mat_in, drv_in,
    e, h, m, back_got,
    mat, drv,
    chunk_a, chunk_b, got_a, got_b,
    hx_send, hx_got, hy_send, hy_got,
    ex_send, ex_got, ey_send, ey_got,
    back,
    load_sem, ready_sem, send_sem, halo_sem, wave_sem, edge_sem, back_sem,
):
    nz, rows, count_x, group, emy, grp = sizes
    tiles = rows // TILE
    film = 3 * FZ
    a = lax.axis_index("emx")
    b = lax.axis_index("emy") * grp + lax.axis_index("grp")

    def peer(index):
        return {"emx": a, "emy": index // grp, "grp": lax.rem(index, grp)}

    a_next, a_prev = lax.rem(a + 1, count_x), lax.rem(a + count_x - 1, count_x)
    b_next, b_prev = lax.rem(b + 1, group), lax.rem(b + group - 1, group)
    to_a_next, to_a_prev = {"emx": a_next}, {"emx": a_prev}
    has_next, has_prev = a < count_x - 1, a > 0
    plane, seat = b // SEATS, lax.rem(b, SEATS)
    far = far_first(group // SEATS)
    same_seat = [(step, 0) for step in far]
    mates = [(0, turn) for turn in range(1, SEATS)]
    others = [(step, turn) for turn in range(1, SEATS) for step in far]

    def member(offset):
        step, turn = offset
        planes = group // SEATS
        return lax.rem(plane + step, planes) * SEATS + lax.rem(seat + turn, SEATS)

    def layers(ref, lo, hi, comp):
        first = (comp * FZ + lo) * rows
        return ref.at[pl.ds(first, (hi - lo) * rows)]

    m_loads = [
        [
            pltpu.make_async_copy(
                layers(m_in, lo, hi, comp), layers(m, lo, hi, comp), load_sem.at[4 + 3 * wave + comp]
            )
            for comp in range(3)
        ]
        for wave, (lo, hi) in enumerate(((0, CUT), (CUT, FZ)))
    ]
    loads = [
        pltpu.make_async_copy(src, dst, load_sem.at[i])
        for i, (src, dst) in enumerate(((h_in, h), (e_in, e), (mat_in, mat), (drv_in, drv)))
    ]

    barrier = pltpu.get_barrier_semaphore()

    def greet(device):
        pl.semaphore_signal(barrier, inc=1, device_id=device, device_id_type=MESH)

    for offset in same_seat + mates:
        greet(peer(member(offset)))

    @pl.when(has_next)
    def _():
        greet(to_a_next)

    @pl.when(has_prev)
    def _():
        greet(to_a_prev)

    for load in m_loads[0] + m_loads[1] + loads:
        load.start()

    lane = lax.broadcasted_iota(jnp.int32, (TILE, LANES), 1)
    wide = lax.broadcasted_iota(jnp.int32, (rows, LANES), 1)
    deep = lax.broadcasted_iota(jnp.int32, (rows, LANES), 0)

    def column(tile, at):
        return jnp.broadcast_to(tile[:, at : at + 1], (TILE, LANES))

    def wait_all(copies):
        for copy in copies:
            copy.wait()

    def place(z):
        return (chunk_a, z) if z < CUT else (chunk_b, z - CUT)

    def fill(lo, hi, lasts, firsts):
        for t in range(tiles):
            for comp in range(3):
                for z in range(lo, hi):
                    q = comp * FZ + z
                    v = m[pl.ds(q * rows + t * TILE, TILE), :]
                    ref, layer = place(z)
                    ref[pl.ds(t * TILE * PITCH + layer * 3 + comp, TILE, stride=PITCH), :] = v
                    lasts[t] = jnp.where(lane == q, column(v, LANES - 1), lasts[t])
                    firsts[t] = jnp.where(lane == film + q, column(v, 0), firsts[t])

    blank = jnp.zeros((TILE, LANES), jnp.float32)
    lasts, firsts = [blank] * tiles, [blank] * tiles
    wait_all(m_loads[0])
    fill(0, CUT, lasts, firsts)
    wait_all(m_loads[1])
    fill(CUT, FZ, lasts, firsts)
    last = jnp.concatenate(lasts, axis=0)
    first = jnp.concatenate(firsts, axis=0)
    last = jnp.where(deep == 0, 0.0, pltpu.roll(last, 1, 0))
    first = jnp.where(deep == rows - 1, 0.0, pltpu.roll(first, rows - 1, 0))
    edges = jnp.where(wide < film, last, first)
    for t in range(tiles):
        chunk_a[pl.ds(t * TILE * PITCH + 3 * CUT, TILE, stride=PITCH), :] = edges[
            t * TILE : (t + 1) * TILE
        ]

    def field(ref, comp, z):
        return ref[pl.ds((comp * nz + z) * rows, rows), :]

    def tile_of(ref, comp, z, t):
        return ref[pl.ds((comp * nz + z) * rows + t * TILE, TILE), :]

    def pack(ref, comps, at):
        packed = jnp.zeros((TILE, LANES), jnp.float32)
        for n, comp in enumerate(comps):
            for z in range(nz):
                for t in range(tiles):
                    v = tile_of(ref, comp, z, t)
                    packed = jnp.where(
                        lane == (n * nz + z) * tiles + t, column(v, at), packed
                    )
        return packed

    def unpack(packed, n, z):
        first = (n * nz + z) * tiles
        return jnp.concatenate([column(packed, first + t) for t in range(tiles)], axis=0)

    loads[0].wait()
    for n, comp in enumerate((1, 2)):
        hx_send[pl.ds(n * nz, nz), :] = h[
            pl.ds(comp * nz * rows + rows - 1, nz, stride=rows), :
        ]
    hy_send[...] = pack(h, (0, 2), LANES - 1)

    def halo(src, dst, which, device):
        return pltpu.make_async_remote_copy(
            src_ref=src,
            dst_ref=dst,
            send_sem=halo_sem.at[0, which],
            recv_sem=halo_sem.at[1, which],
            device_id=device,
            device_id_type=MESH,
        )

    def go(copy, sends):
        @pl.when(sends)
        def _():
            copy.start()

    def land(copy, sends, receives):
        @pl.when(receives)
        def _():
            copy.wait_recv()

        @pl.when(sends)
        def _():
            copy.wait_send()

    def block(ref, index, size):
        return ref.at[pl.ds(pl.multiple_of(index * PITCH, PITCH), size)]

    hx = halo(hx_send, hx_got, 0, to_a_next)
    hy = halo(hy_send, hy_got, 1, peer(b_next))
    kind = (b + group - 2) // (group - 1) + b // (group - 1)
    waves = ((chunk_a, got_a, 3 * CUT + 1), (chunk_b, got_b, 3 * (FZ - CUT)))

    def send_wave(wave, part):
        src, dst, size = waves[wave]
        for offset in part:
            j = member(offset)
            pltpu.make_async_remote_copy(
                src_ref=block(src, j, size),
                dst_ref=block(dst, b + 1, size),
                send_sem=send_sem.at[wave],
                recv_sem=wave_sem.at[wave, kind],
                device_id=peer(j),
                device_id_type=MESH,
            ).start()

    for wave, (src, dst, size) in enumerate(waves):
        pltpu.make_async_copy(
            block(src, b, size), block(dst, b + 1, size), wave_sem.at[wave, kind]
        ).start()
    pl.semaphore_wait(
        barrier, len(same_seat + mates) + jnp.int32(has_next) + jnp.int32(has_prev)
    )
    for offset in mates:
        pl.semaphore_signal(
            ready_sem, inc=1, device_id=peer(member(offset)), device_id_type=MESH
        )
    send_wave(0, same_seat)
    pl.semaphore_wait(ready_sem, len(mates))
    go(hx, has_next)
    hy.start()
    send_wave(0, others + mates)

    @pl.when(b == rows - 1)
    def _():
        send_wave(1, same_seat + others + mates)


    for load in loads[1:]:
        load.wait()
    index_x = a * rows + deep
    index_y = b * LANES + wide
    sigma = grade(index_x, count_x * rows) + grade(index_y, group * LANES)
    decay = (1.0 - sigma) / (1.0 + sigma)
    hstep = step_dt / (1.0 + sigma)
    film_step = step_dt / (film_eps * (1.0 + sigma))
    material = mat[...]
    eps = jnp.where(
        material == 0, 1.0, jnp.where(material == 1, 2.2, jnp.where(material == 2, 4.4, 9.8))
    ).astype(jnp.float32)
    upper_step = step_dt / (eps * (1.0 + sigma))

    land(hx, has_next, has_prev)
    hy.wait()
    left = jnp.where(b == 0, 0.0, hy_got[...])

    def below_x(v, n, z):
        edge = jnp.where(has_prev, hx_got[pl.ds(n * nz + z, 1), :], 0.0)
        return jnp.where(deep == 0, edge, pltpu.roll(v, 1, 0))

    def below_y(v, n, z):
        return jnp.where(wide == 0, unpack(left, n, z), pltpu.roll(v, 1, 1))

    under = None
    for z in range(nz):
        hx_z, hy_z, hz_z = (field(h, comp, z) for comp in range(3))
        back_zy = hz_z - below_y(hz_z, 1, z)
        back_zx = hz_z - below_x(hz_z, 1, z)
        back_yx = hy_z - below_x(hy_z, 0, z)
        back_xy = hx_z - below_y(hx_z, 0, z)
        back_yz = hy_z if under is None else hy_z - under[1]
        back_xz = hx_z if under is None else hx_z - under[0]
        comp_x = back_zy - back_yz
        if z == nz - 1:
            comp_x = comp_x - drv[...]
        comp_y = back_xz - back_zx
        comp_z = back_yx - back_xy
        estep = film_step if z < FZ else upper_step
        for comp, value in enumerate((comp_x, comp_y, comp_z)):
            e[pl.ds((comp * nz + z) * rows, rows), :] = decay * field(e, comp, z) + estep * value
        under = (hx_z, hy_z)

    for n, comp in enumerate((1, 2)):
        ex_send[pl.ds(n * nz, nz), :] = e[pl.ds(comp * nz * rows, nz, stride=rows), :]
    ey_send[...] = pack(e, (0, 2), 0)
    ex = halo(ex_send, ex_got, 2, to_a_prev)
    ey = halo(ey_send, ey_got, 3, peer(b_prev))
    go(ex, has_prev)
    ey.start()

    @pl.when(b != rows - 1)
    def _():
        send_wave(1, same_seat + others + mates)

    def wait_wave(wave, which, count):
        _, dst, size = waves[wave]
        landed = dst.at[pl.ds(0, count * size)]
        pltpu.make_async_copy(landed, landed, wave_sem.at[wave, which]).wait()

    def edge(wave, src, dst, which, device):
        _, ref, size = waves[wave]
        return pltpu.make_async_remote_copy(
            src_ref=block(ref, src, size),
            dst_ref=block(ref, dst, size),
            send_sem=edge_sem.at[0, wave, which],
            recv_sem=edge_sem.at[1, wave, which],
            device_id=device,
            device_id_type=MESH,
        )

    high = [edge(wave, rows, 0, 1, to_a_next) for wave in range(2)]
    low = [edge(wave, 1, rows + 1, 0, to_a_prev) for wave in range(2)]

    def pass_high(wave):
        wait_wave(wave, 2, 1)
        go(high[wave], has_next)

    def pass_low(wave):
        wait_wave(wave, 0, 1)
        go(low[wave], has_prev)

    pass_high(0)
    pass_low(0)

    land(ex, has_prev, has_next)
    ey.wait()
    right = jnp.where(b == group - 1, 0.0, ey_got[...])

    def above_x(v, n, z):
        edge = jnp.where(has_next, ex_got[pl.ds(n * nz + z, 1), :], 0.0)
        return jnp.where(deep == rows - 1, edge, pltpu.roll(v, rows - 1, 0))

    def above_y(v, n, z):
        return jnp.where(wide == LANES - 1, unpack(right, n, z), pltpu.roll(v, LANES - 1, 1))

    for z in range(nz):
        ex_z, ey_z, ez_z = (field(e, comp, z) for comp in range(3))
        fore_zy = above_y(ez_z, 1, z) - ez_z
        fore_zx = above_x(ez_z, 1, z) - ez_z
        fore_yx = above_x(ey_z, 0, z) - ey_z
        fore_xy = above_y(ex_z, 0, z) - ex_z
        fore_yz = (field(e, 1, z + 1) if z < nz - 1 else 0.0) - ey_z
        fore_xz = (field(e, 0, z + 1) if z < nz - 1 else 0.0) - ex_z
        curls = (fore_zy - fore_yz, fore_xz - fore_zx, fore_yx - fore_xy)
        for comp, value in enumerate(curls):
            h[pl.ds((comp * nz + z) * rows, rows), :] = decay * field(h, comp, z) - hstep * value

    def spin(first, count, stride, half):
        def take(ref, base, pitch):
            return ref[pl.ds(base, count, stride=pitch), :]

        sides = take(got_a, (first + 1) * PITCH + 3 * CUT, stride * PITCH)
        lane = lax.broadcasted_iota(jnp.int32, (count, LANES), 1)

        def column(tile, at):
            return jnp.broadcast_to(tile[:, at : at + 1], (count, LANES))

        def spins(comp, z, shift):
            ref, layer = (got_a, z) if z < CUT else (got_b, z - CUT)
            return take(ref, (first + 1 + shift) * PITCH + layer * 3 + comp, stride * PITCH)

        for layer in range(HALF):
            z = half * HALF + layer
            centre = [spins(comp, z, 0) for comp in range(3)]
            heff = []
            for comp in range(3):
                v = centre[comp]
                q = comp * FZ + z
                y_up = jnp.where(
                    lane == LANES - 1, column(sides, film + q), pltpu.roll(v, LANES - 1, 1)
                )
                y_down = jnp.where(lane == 0, column(sides, q), pltpu.roll(v, 1, 1))
                lap = spins(comp, z, 1) + spins(comp, z, -1) + y_up + y_down
                if z < FZ - 1:
                    lap = lap + spins(comp, z + 1, 0)
                if z > 0:
                    lap = lap + spins(comp, z - 1, 0)
                lap = lap - 6.0 * v
                value = take(h, (comp * nz + z) * rows + first, stride) + exch_coef * lap
                if comp == 2:
                    value = value + 1.0 + 0.5 * v
                heff.append(value)
            mx, my, mz = centre
            tx = my * heff[2] - mz * heff[1]
            ty = mz * heff[0] - mx * heff[2]
            tz = mx * heff[1] - my * heff[0]
            dx = -gyro_coef * (tx + damp_coef * (my * tz - mz * ty))
            dy = -gyro_coef * (ty + damp_coef * (mz * tx - mx * tz))
            dz = -gyro_coef * (tz + damp_coef * (mx * ty - my * tx))
            for comp, d in enumerate((dx, dy, dz)):
                at = pl.ds((comp * nz + z) * rows + first, count, stride=stride)
                h[at, :] = h[at, :] - d
            big_x, big_y = largest(mx, my, mz)
            u = jnp.where(big_x, dy, jnp.where(big_y, dz, dx))
            v = jnp.where(big_x, dz, jnp.where(big_y, dx, dy))
            at = (half * rows + first) * 2 * HALF + 2 * layer
            back[pl.ds(at, count, stride=stride * 2 * HALF), :] = u
            back[pl.ds(at + 1, count, stride=stride * 2 * HALF), :] = v

    def part(ref, half, index):
        first = (half * group + index) * 2 * HALF
        return ref.at[pl.ds(pl.multiple_of(first, 2 * HALF), 2 * HALF)]

    def send_back(indices, half):
        for i in indices:

            @pl.when(b != i)
            def _():
                pltpu.make_async_remote_copy(
                    src_ref=part(back, half, i),
                    dst_ref=part(back_got, half, b),
                    send_sem=send_sem.at[2 + half],
                    recv_sem=back_sem.at[half],
                    device_id={"emx": a, "emy": i // grp, "grp": i % grp},
                    device_id_type=MESH,
                ).start()

            @pl.when(b == i)
            def _():
                pltpu.make_async_copy(
                    part(back, half, i), part(back_got, half, b), back_sem.at[half]
                ).start()

    def work(half, lo, hi):
        for first in range(lo, hi, TILE):
            spin(first, min(TILE, hi - first), 1, half)

        def within(row):
            return jnp.logical_and(row >= lo, row < hi)

        for offset in everyone:
            row = member(offset)

            @pl.when(within(row))
            def _():
                pltpu.make_async_remote_copy(
                    src_ref=part(back, half, row),
                    dst_ref=part(back_got, half, b),
                    send_sem=send_sem.at[2 + half],
                    recv_sem=back_sem.at[half],
                    device_id=peer(row),
                    device_id_type=MESH,
                ).start()

        @pl.when(within(b))
        def _():
            pltpu.make_async_copy(
                part(back, half, b), part(back_got, half, b), back_sem.at[half]
            ).start()

    everyone = [(step, turn) for step in far for turn in range(SEATS)] + mates

    def inner(half, lo, hi):
        for first in range(lo, hi, TILE):
            count = min(TILE, hi - first)
            spin(first, count, 1, half)
            send_back(range(first, first + count), half)

    def outer(half, row):
        ref = waves[half][1]
        if row == 0:
            land(high[half], has_next, has_prev)
            known, ghost = has_prev, 0
        else:
            land(low[half], has_prev, has_next)
            known, ghost = has_next, rows + 1

        @pl.when(jnp.logical_not(known))
        def _():
            ref[pl.ds(ghost * PITCH, PITCH), :] = jnp.zeros((PITCH, LANES), jnp.float32)

        spin(row, 1, 1, half)
        send_back((row,), half)

    cuts = [min(cut, rows - 1) for cut in CUTS]
    wait_wave(0, 1, rows - 2)
    inner(0, 1, cuts[0])
    pass_high(1)
    inner(0, cuts[0], cuts[1])
    outer(0, 0)
    inner(0, cuts[1], rows - 1)
    pass_low(1)
    outer(0, rows - 1)
    early = rows // 2
    wait_wave(1, 1, rows - 2)
    work(1, 1, rows // 4)
    outer(1, 0)
    work(1, rows // 4, early)
    work(1, early, rows - 1)
    outer(1, rows - 1)
    for half in range(2):
        landed = back_got.at[pl.ds(half * group * 2 * HALF, group * 2 * HALF)]
        pltpu.make_async_copy(landed, landed, back_sem.at[half]).wait()
        if half == 0:
            turn_magnet(m, back_got, group, half)

    for sem, size in enumerate((3 * CUT + 1, 3 * (FZ - CUT), 2 * HALF, 2 * HALF)):
        sent = chunk_a.at[pl.ds(0, (group - 1) * size)]
        pltpu.make_async_copy(sent, sent, send_sem.at[sem]).wait()


def turn_magnet(m, back_got, rows, half):
    for t in range(rows // TILE):
        for layer in range(HALF):
            z = half * HALF + layer
            places = [pl.ds((comp * FZ + z) * rows + t * TILE, TILE) for comp in range(3)]
            mx, my, mz = (m[at, :] for at in places)
            at = (half * rows + t * TILE) * 2 * HALF + 2 * layer
            u = back_got[pl.ds(at, TILE, stride=2 * HALF), :]
            v = back_got[pl.ds(at + 1, TILE, stride=2 * HALF), :]
            big_x, big_y = largest(mx, my, mz)
            big = jnp.where(big_x, mx, jnp.where(big_y, my, mz))
            mu = jnp.where(big_x, my, jnp.where(big_y, mz, mx))
            mv = jnp.where(big_x, mz, jnp.where(big_y, mx, my))
            tiny = jnp.abs(big) < 1e-30
            scale = jnp.where(tiny, 0.0, 1.0 / jnp.where(tiny, 1.0, big))
            w = -((mu * scale) * u + (mv * scale) * v)
            m[places[0], :] = mx + jnp.where(big_x, w, jnp.where(big_y, v, u))
            m[places[1], :] = my + jnp.where(big_x, u, jnp.where(big_y, w, v))
            m[places[2], :] = mz + jnp.where(big_x, v, jnp.where(big_y, u, w))


def store_kernel(rows, e, h, m, back_got, e_out, h_out, m_out, part, sem):
    size = HALF * rows
    copies = [
        pltpu.make_async_copy(src, dst, sem.at[i]) for i, (src, dst) in enumerate(((e, e_out), (h, h_out)))
    ]
    for comp in range(3):
        at = pl.ds(comp * FZ * rows, size)
        copies.append(pltpu.make_async_copy(m.at[at], m_out.at[at], sem.at[2 + comp]))
    for copy in copies:
        copy.start()
    for comp in range(3):
        part[pl.ds((comp * FZ + HALF) * rows, size), :] = m[pl.ds((comp * FZ + HALF) * rows, size), :]
    turn_magnet(part, back_got, rows, 1)
    for comp in range(3):
        at = pl.ds((comp * FZ + HALF) * rows, size)
        copy = pltpu.make_async_copy(part.at[at], m_out.at[at], sem.at[5 + comp])
        copy.start()
        copies.append(copy)
    for copy in copies:
        copy.wait()


def largest(mx, my, mz):
    sx, sy, sz = jnp.abs(mx), jnp.abs(my), jnp.abs(mz)
    big_x = (sx >= sy) & (sx >= sz)
    big_y = sy >= sz
    return big_x, big_y


def shards(efield, hfield, magnet, material, drive):
    _, nz, rows, cols_y = efield.shape
    count_x = lax.axis_size("emx")
    emy, grp = lax.axis_size("emy"), lax.axis_size("grp")
    group = emy * grp
    assert cols_y == LANES and rows == group and magnet.shape[2] == 1
    film = 3 * FZ
    tiles = rows // TILE
    assert 2 * nz * tiles <= LANES and 2 * film <= LANES
    f32 = jnp.float32
    field_shape = (3 * nz * rows, LANES)
    spin_shape = (film * group, LANES)
    dma = pltpu.SemaphoreType.DMA
    any_spec = pl.BlockSpec(memory_space=pl.ANY)
    sizes = (nz, rows, count_x, group, emy, grp)
    vmem_spec = pl.BlockSpec(memory_space=pltpu.VMEM)
    operands = [
        pltpu.with_memory_space_constraint(operand, pltpu.HBM)
        for operand in (
            efield.reshape(field_shape),
            hfield.reshape(field_shape),
            magnet.reshape(spin_shape),
            material,
            drive,
        )
    ]
    held = pl.pallas_call(
        functools.partial(step_kernel, sizes),
        out_shape=(
            pltpu.VMEM(field_shape, f32),
            pltpu.VMEM(field_shape, f32),
            pltpu.VMEM(spin_shape, f32),
            pltpu.VMEM((group * 2 * FZ, LANES), f32),
        ),
        in_specs=[any_spec] * 5,
        out_specs=[vmem_spec] * 4,
        scratch_shapes=[
            pltpu.VMEM((rows, LANES), jnp.int32),
            pltpu.VMEM((rows, LANES), f32),
            pltpu.VMEM((group * PITCH, LANES), f32),
            pltpu.VMEM((group * PITCH, LANES), f32),
            pltpu.VMEM(((rows + 2) * PITCH, LANES), f32),
            pltpu.VMEM(((rows + 2) * PITCH, LANES), f32),
            pltpu.VMEM((2 * nz, LANES), f32),
            pltpu.VMEM((2 * nz, LANES), f32),
            pltpu.VMEM((TILE, LANES), f32),
            pltpu.VMEM((TILE, LANES), f32),
            pltpu.VMEM((2 * nz, LANES), f32),
            pltpu.VMEM((2 * nz, LANES), f32),
            pltpu.VMEM((TILE, LANES), f32),
            pltpu.VMEM((TILE, LANES), f32),
            pltpu.VMEM((rows * 2 * FZ, LANES), f32),
            dma((10,)),
            pltpu.SemaphoreType.REGULAR,
            dma((4,)),
            dma((2, 4)),
            dma((2, 3)),
            dma((2, 2, 2)),
            dma((2,)),
        ],
        compiler_params=pltpu.CompilerParams(
            collective_id=0, has_side_effects=True, vmem_limit_bytes=32 * 1024 * 1024
        ),
    )(*operands)
    outs = pl.pallas_call(
        functools.partial(store_kernel, rows),
        out_shape=(
            jax.ShapeDtypeStruct(field_shape, f32),
            jax.ShapeDtypeStruct(field_shape, f32),
            jax.ShapeDtypeStruct(spin_shape, f32),
        ),
        in_specs=[vmem_spec] * 4,
        out_specs=[any_spec] * 3,
        scratch_shapes=[pltpu.VMEM(spin_shape, f32), dma((8,))],
    )(*(pltpu.with_memory_space_constraint(part, pltpu.VMEM) for part in held))
    return (
        outs[0].reshape(efield.shape),
        outs[1].reshape(hfield.shape),
        outs[2].reshape(magnet.shape),
    )


def solution(mesh):
    return jax.shard_map(
        shards,
        mesh=mesh,
        in_specs=(
            P(None, None, "emx", ("emy", "grp")),
            P(None, None, "emx", ("emy", "grp")),
            P(None, None, ("emx", "emy", "grp"), None),
            P("emx", ("emy", "grp")),
            P("emx", ("emy", "grp")),
        ),
        out_specs=(
            P(None, None, "emx", ("emy", "grp")),
            P(None, None, "emx", ("emy", "grp")),
            P(None, None, ("emx", "emy", "grp"), None),
        ),
        check_vma=False,
    )
```

```python
import functools

import jax
import jax.numpy as jnp
from jax import lax
from jax.experimental import pallas as pl
from jax.experimental.pallas import tpu as pltpu
from jax.sharding import PartitionSpec as P

FZ = 8
W = 8

step_dt = 0.5
film_eps = 15.0
exch_coef = 0.25
gyro_coef = 0.3
damp_coef = 0.1

MESH = pl.DeviceIdType.MESH
LANES = 128
CUT = 5
HALF = FZ // 2
PITCH = 16
SEATS = 4
CUTS = (9, 25, 9)
TILE = 8


def grade(index, count):
    edge = jnp.minimum(index, count - 1 - index)
    depth = jnp.maximum(W - edge, 0).astype(jnp.float32) / W
    return 0.4 * depth * depth


def far_first(count):
    return sorted(range(1, count), key=lambda step: -min(step, count - step))


def step_kernel(
    sizes,
    e_in, h_in, m_in, mat_in, drv_in,
    e, h, m, back_got,
    mat, drv,
    chunk_a, chunk_b, got_a, got_b,
    hx_send, hx_got, hy_send, hy_got,
    ex_send, ex_got, ey_send, ey_got,
    back,
    load_sem, ready_sem, send_sem, halo_sem, wave_sem, edge_sem, back_sem,
):
    nz, rows, count_x, group, emy, grp = sizes
    tiles = rows // TILE
    film = 3 * FZ
    a = lax.axis_index("emx")
    b = lax.axis_index("emy") * grp + lax.axis_index("grp")

    def peer(index):
        return {"emx": a, "emy": index // grp, "grp": lax.rem(index, grp)}

    a_next, a_prev = lax.rem(a + 1, count_x), lax.rem(a + count_x - 1, count_x)
    b_next, b_prev = lax.rem(b + 1, group), lax.rem(b + group - 1, group)
    to_a_next, to_a_prev = {"emx": a_next}, {"emx": a_prev}
    has_next, has_prev = a < count_x - 1, a > 0
    plane, seat = b // SEATS, lax.rem(b, SEATS)
    far = far_first(group // SEATS)
    same_seat = [(step, 0) for step in far]
    mates = [(0, turn) for turn in range(1, SEATS)]
    others = [(step, turn) for turn in range(1, SEATS) for step in far]

    def member(offset):
        step, turn = offset
        planes = group // SEATS
        return lax.rem(plane + step, planes) * SEATS + lax.rem(seat + turn, SEATS)

    def layers(ref, lo, hi, comp):
        first = (comp * FZ + lo) * rows
        return ref.at[pl.ds(first, (hi - lo) * rows)]

    m_loads = [
        [
            pltpu.make_async_copy(
                layers(m_in, lo, hi, comp), layers(m, lo, hi, comp), load_sem.at[4 + 3 * wave + comp]
            )
            for comp in range(3)
        ]
        for wave, (lo, hi) in enumerate(((0, CUT), (CUT, FZ)))
    ]
    loads = [
        pltpu.make_async_copy(src, dst, load_sem.at[i])
        for i, (src, dst) in enumerate(((h_in, h), (e_in, e), (mat_in, mat), (drv_in, drv)))
    ]

    barrier = pltpu.get_barrier_semaphore()

    def greet(device):
        pl.semaphore_signal(barrier, inc=1, device_id=device, device_id_type=MESH)

    for offset in same_seat + mates:
        greet(peer(member(offset)))

    @pl.when(has_next)
    def _():
        greet(to_a_next)

    @pl.when(has_prev)
    def _():
        greet(to_a_prev)

    for load in m_loads[0] + m_loads[1] + loads:
        load.start()

    lane = lax.broadcasted_iota(jnp.int32, (TILE, LANES), 1)
    wide = lax.broadcasted_iota(jnp.int32, (rows, LANES), 1)
    deep = lax.broadcasted_iota(jnp.int32, (rows, LANES), 0)

    def column(tile, at):
        return jnp.broadcast_to(tile[:, at : at + 1], (TILE, LANES))

    def wait_all(copies):
        for copy in copies:
            copy.wait()

    def place(z):
        return (chunk_a, z) if z < CUT else (chunk_b, z - CUT)

    def fill(lo, hi, lasts, firsts):
        for t in range(tiles):
            for comp in range(3):
                for z in range(lo, hi):
                    q = comp * FZ + z
                    v = m[pl.ds(q * rows + t * TILE, TILE), :]
                    ref, layer = place(z)
                    ref[pl.ds(t * TILE * PITCH + layer * 3 + comp, TILE, stride=PITCH), :] = v
                    lasts[t] = jnp.where(lane == q, column(v, LANES - 1), lasts[t])
                    firsts[t] = jnp.where(lane == film + q, column(v, 0), firsts[t])

    blank = jnp.zeros((TILE, LANES), jnp.float32)
    lasts, firsts = [blank] * tiles, [blank] * tiles
    wait_all(m_loads[0])
    fill(0, CUT, lasts, firsts)
    wait_all(m_loads[1])
    fill(CUT, FZ, lasts, firsts)
    last = jnp.concatenate(lasts, axis=0)
    first = jnp.concatenate(firsts, axis=0)
    last = jnp.where(deep == 0, 0.0, pltpu.roll(last, 1, 0))
    first = jnp.where(deep == rows - 1, 0.0, pltpu.roll(first, rows - 1, 0))
    edges = jnp.where(wide < film, last, first)
    for t in range(tiles):
        chunk_a[pl.ds(t * TILE * PITCH + 3 * CUT, TILE, stride=PITCH), :] = edges[
            t * TILE : (t + 1) * TILE
        ]

    def field(ref, comp, z):
        return ref[pl.ds((comp * nz + z) * rows, rows), :]

    def tile_of(ref, comp, z, t):
        return ref[pl.ds((comp * nz + z) * rows + t * TILE, TILE), :]

    def pack(ref, comps, at):
        packed = jnp.zeros((TILE, LANES), jnp.float32)
        for n, comp in enumerate(comps):
            for z in range(nz):
                for t in range(tiles):
                    v = tile_of(ref, comp, z, t)
                    packed = jnp.where(
                        lane == (n * nz + z) * tiles + t, column(v, at), packed
                    )
        return packed

    def unpack(packed, n, z):
        first = (n * nz + z) * tiles
        return jnp.concatenate([column(packed, first + t) for t in range(tiles)], axis=0)

    loads[0].wait()
    for n, comp in enumerate((1, 2)):
        hx_send[pl.ds(n * nz, nz), :] = h[
            pl.ds(comp * nz * rows + rows - 1, nz, stride=rows), :
        ]
    hy_send[...] = pack(h, (0, 2), LANES - 1)

    def halo(src, dst, which, device):
        return pltpu.make_async_remote_copy(
            src_ref=src,
            dst_ref=dst,
            send_sem=halo_sem.at[0, which],
            recv_sem=halo_sem.at[1, which],
            device_id=device,
            device_id_type=MESH,
        )

    def go(copy, sends):
        @pl.when(sends)
        def _():
            copy.start()

    pending = []

    def land(copy, sends, receives):
        @pl.when(receives)
        def _():
            copy.wait_recv()

        pending.append((copy, sends))

    def block(ref, index, size):
        return ref.at[pl.ds(pl.multiple_of(index * PITCH, PITCH), size)]

    hx = halo(hx_send, hx_got, 0, to_a_next)
    hy = halo(hy_send, hy_got, 1, peer(b_next))
    kind = (b + group - 2) // (group - 1) + b // (group - 1)
    waves = ((chunk_a, got_a, 3 * CUT + 1), (chunk_b, got_b, 3 * (FZ - CUT)))

    def send_wave(wave, part):
        src, dst, size = waves[wave]
        for offset in part:
            j = member(offset)
            pltpu.make_async_remote_copy(
                src_ref=block(src, j, size),
                dst_ref=block(dst, b + 1, size),
                send_sem=send_sem.at[wave],
                recv_sem=wave_sem.at[wave, kind],
                device_id=peer(j),
                device_id_type=MESH,
            ).start()

    for wave, (src, dst, size) in enumerate(waves):
        pltpu.make_async_copy(
            block(src, b, size), block(dst, b + 1, size), wave_sem.at[wave, kind]
        ).start()
    pl.semaphore_wait(
        barrier, len(same_seat + mates) + jnp.int32(has_next) + jnp.int32(has_prev)
    )
    for offset in mates:
        pl.semaphore_signal(
            ready_sem, inc=1, device_id=peer(member(offset)), device_id_type=MESH
        )
    send_wave(0, same_seat)
    pl.semaphore_wait(ready_sem, len(mates))
    go(hx, has_next)
    hy.start()
    send_wave(0, others + mates)

    @pl.when(b == rows - 1)
    def _():
        send_wave(1, same_seat + others + mates)


    for load in loads[1:]:
        load.wait()
    index_x = a * rows + deep
    index_y = b * LANES + wide
    sigma = grade(index_x, count_x * rows) + grade(index_y, group * LANES)
    decay = (1.0 - sigma) / (1.0 + sigma)
    hstep = step_dt / (1.0 + sigma)
    film_step = step_dt / (film_eps * (1.0 + sigma))
    material = mat[...]
    eps = jnp.where(
        material == 0, 1.0, jnp.where(material == 1, 2.2, jnp.where(material == 2, 4.4, 9.8))
    ).astype(jnp.float32)
    upper_step = step_dt / (eps * (1.0 + sigma))

    land(hx, has_next, has_prev)
    hy.wait_recv()
    left = jnp.where(b == 0, 0.0, hy_got[...])

    def below_x(v, n, z):
        edge = jnp.where(has_prev, hx_got[pl.ds(n * nz + z, 1), :], 0.0)
        return jnp.where(deep == 0, edge, pltpu.roll(v, 1, 0))

    def below_y(v, n, z):
        return jnp.where(wide == 0, unpack(left, n, z), pltpu.roll(v, 1, 1))

    under = None
    for z in range(nz):
        hx_z, hy_z, hz_z = (field(h, comp, z) for comp in range(3))
        back_zy = hz_z - below_y(hz_z, 1, z)
        back_zx = hz_z - below_x(hz_z, 1, z)
        back_yx = hy_z - below_x(hy_z, 0, z)
        back_xy = hx_z - below_y(hx_z, 0, z)
        back_yz = hy_z if under is None else hy_z - under[1]
        back_xz = hx_z if under is None else hx_z - under[0]
        comp_x = back_zy - back_yz
        if z == nz - 1:
            comp_x = comp_x - drv[...]
        comp_y = back_xz - back_zx
        comp_z = back_yx - back_xy
        estep = film_step if z < FZ else upper_step
        for comp, value in enumerate((comp_x, comp_y, comp_z)):
            e[pl.ds((comp * nz + z) * rows, rows), :] = decay * field(e, comp, z) + estep * value
        under = (hx_z, hy_z)

    for n, comp in enumerate((1, 2)):
        ex_send[pl.ds(n * nz, nz), :] = e[pl.ds(comp * nz * rows, nz, stride=rows), :]
    ey_send[...] = pack(e, (0, 2), 0)
    ex = halo(ex_send, ex_got, 2, to_a_prev)
    ey = halo(ey_send, ey_got, 3, peer(b_prev))
    go(ex, has_prev)
    ey.start()

    @pl.when(b != rows - 1)
    def _():
        send_wave(1, same_seat + others + mates)

    def wait_wave(wave, which, count):
        _, dst, size = waves[wave]
        landed = dst.at[pl.ds(0, count * size)]
        pltpu.make_async_copy(landed, landed, wave_sem.at[wave, which]).wait()

    def edge(wave, src, dst, which, device):
        _, ref, size = waves[wave]
        return pltpu.make_async_remote_copy(
            src_ref=block(ref, src, size),
            dst_ref=block(ref, dst, size),
            send_sem=edge_sem.at[0, wave, which],
            recv_sem=edge_sem.at[1, wave, which],
            device_id=device,
            device_id_type=MESH,
        )

    high = [edge(wave, rows, 0, 1, to_a_next) for wave in range(2)]
    low = [edge(wave, 1, rows + 1, 0, to_a_prev) for wave in range(2)]

    def pass_high(wave):
        wait_wave(wave, 2, 1)
        go(high[wave], has_next)

    def pass_low(wave):
        wait_wave(wave, 0, 1)
        go(low[wave], has_prev)

    pass_high(0)
    pass_low(0)

    land(ex, has_prev, has_next)
    ey.wait_recv()
    right = jnp.where(b == group - 1, 0.0, ey_got[...])

    def above_x(v, n, z):
        edge = jnp.where(has_next, ex_got[pl.ds(n * nz + z, 1), :], 0.0)
        return jnp.where(deep == rows - 1, edge, pltpu.roll(v, rows - 1, 0))

    def above_y(v, n, z):
        return jnp.where(wide == LANES - 1, unpack(right, n, z), pltpu.roll(v, LANES - 1, 1))

    for z in range(nz):
        ex_z, ey_z, ez_z = (field(e, comp, z) for comp in range(3))
        fore_zy = above_y(ez_z, 1, z) - ez_z
        fore_zx = above_x(ez_z, 1, z) - ez_z
        fore_yx = above_x(ey_z, 0, z) - ey_z
        fore_xy = above_y(ex_z, 0, z) - ex_z
        fore_yz = (field(e, 1, z + 1) if z < nz - 1 else 0.0) - ey_z
        fore_xz = (field(e, 0, z + 1) if z < nz - 1 else 0.0) - ex_z
        curls = (fore_zy - fore_yz, fore_xz - fore_zx, fore_yx - fore_xy)
        for comp, value in enumerate(curls):
            h[pl.ds((comp * nz + z) * rows, rows), :] = decay * field(h, comp, z) - hstep * value

    def spin(first, count, stride, half):
        def take(ref, base, pitch):
            return ref[pl.ds(base, count, stride=pitch), :]

        sides = take(got_a, (first + 1) * PITCH + 3 * CUT, stride * PITCH)
        lane = lax.broadcasted_iota(jnp.int32, (count, LANES), 1)

        def column(tile, at):
            return jnp.broadcast_to(tile[:, at : at + 1], (count, LANES))

        def spins(comp, z, shift):
            ref, layer = (got_a, z) if z < CUT else (got_b, z - CUT)
            return take(ref, (first + 1 + shift) * PITCH + layer * 3 + comp, stride * PITCH)

        for layer in range(HALF):
            z = half * HALF + layer
            centre = [spins(comp, z, 0) for comp in range(3)]
            heff = []
            for comp in range(3):
                v = centre[comp]
                q = comp * FZ + z
                y_up = jnp.where(
                    lane == LANES - 1, column(sides, film + q), pltpu.roll(v, LANES - 1, 1)
                )
                y_down = jnp.where(lane == 0, column(sides, q), pltpu.roll(v, 1, 1))
                lap = spins(comp, z, 1) + spins(comp, z, -1) + y_up + y_down
                if z < FZ - 1:
                    lap = lap + spins(comp, z + 1, 0)
                if z > 0:
                    lap = lap + spins(comp, z - 1, 0)
                lap = lap - 6.0 * v
                value = take(h, (comp * nz + z) * rows + first, stride) + exch_coef * lap
                if comp == 2:
                    value = value + 1.0 + 0.5 * v
                heff.append(value)
            mx, my, mz = centre
            tx = my * heff[2] - mz * heff[1]
            ty = mz * heff[0] - mx * heff[2]
            tz = mx * heff[1] - my * heff[0]
            dx = -gyro_coef * (tx + damp_coef * (my * tz - mz * ty))
            dy = -gyro_coef * (ty + damp_coef * (mz * tx - mx * tz))
            dz = -gyro_coef * (tz + damp_coef * (mx * ty - my * tx))
            for comp, d in enumerate((dx, dy, dz)):
                at = pl.ds((comp * nz + z) * rows + first, count, stride=stride)
                h[at, :] = h[at, :] - d
            big_x, big_y = largest(mx, my, mz)
            u = jnp.where(big_x, dy, jnp.where(big_y, dz, dx))
            v = jnp.where(big_x, dz, jnp.where(big_y, dx, dy))
            at = (half * rows + first) * 2 * HALF + 2 * layer
            back[pl.ds(at, count, stride=stride * 2 * HALF), :] = u
            back[pl.ds(at + 1, count, stride=stride * 2 * HALF), :] = v

    def part(ref, half, index):
        first = (half * group + index) * 2 * HALF
        return ref.at[pl.ds(pl.multiple_of(first, 2 * HALF), 2 * HALF)]

    def send_back(indices, half):
        for i in indices:

            @pl.when(b != i)
            def _():
                pltpu.make_async_remote_copy(
                    src_ref=part(back, half, i),
                    dst_ref=part(back_got, half, b),
                    send_sem=send_sem.at[2 + half],
                    recv_sem=back_sem.at[half],
                    device_id={"emx": a, "emy": i // grp, "grp": i % grp},
                    device_id_type=MESH,
                ).start()

            @pl.when(b == i)
            def _():
                pltpu.make_async_copy(
                    part(back, half, i), part(back_got, half, b), back_sem.at[half]
                ).start()

    def work(half, lo, hi):
        for first in range(lo, hi, TILE):
            spin(first, min(TILE, hi - first), 1, half)

        def within(row):
            return jnp.logical_and(row >= lo, row < hi)

        for offset in everyone:
            row = member(offset)

            @pl.when(within(row))
            def _():
                pltpu.make_async_remote_copy(
                    src_ref=part(back, half, row),
                    dst_ref=part(back_got, half, b),
                    send_sem=send_sem.at[2 + half],
                    recv_sem=back_sem.at[half],
                    device_id=peer(row),
                    device_id_type=MESH,
                ).start()

        @pl.when(within(b))
        def _():
            pltpu.make_async_copy(
                part(back, half, b), part(back_got, half, b), back_sem.at[half]
            ).start()

    everyone = [(step, turn) for step in far for turn in range(SEATS)] + mates

    def inner(half, lo, hi):
        for first in range(lo, hi, TILE):
            count = min(TILE, hi - first)
            spin(first, count, 1, half)
            send_back(range(first, first + count), half)

    def outer(half, row):
        ref = waves[half][1]
        if row == 0:
            land(high[half], has_next, has_prev)
            known, ghost = has_prev, 0
        else:
            land(low[half], has_prev, has_next)
            known, ghost = has_next, rows + 1

        @pl.when(jnp.logical_not(known))
        def _():
            ref[pl.ds(ghost * PITCH, PITCH), :] = jnp.zeros((PITCH, LANES), jnp.float32)

        spin(row, 1, 1, half)
        send_back((row,), half)

    cuts = [min(cut, rows - 1) for cut in CUTS]
    wait_wave(0, 1, rows - 2)
    inner(0, 1, cuts[0])
    pass_high(1)
    inner(0, cuts[0], cuts[1])
    outer(0, 0)
    inner(0, cuts[1], rows - 1)
    pass_low(1)
    outer(0, rows - 1)
    early = rows // 2
    wait_wave(1, 1, rows - 2)
    work(1, 1, rows // 4)
    outer(1, 0)
    work(1, rows // 4, early)
    work(1, early, rows - 1)
    outer(1, rows - 1)
    for half in range(2):
        landed = back_got.at[pl.ds(half * group * 2 * HALF, group * 2 * HALF)]
        pltpu.make_async_copy(landed, landed, back_sem.at[half]).wait()
        if half == 0:
            turn_magnet(m, back_got, group, half)

    hy.wait_send()
    ey.wait_send()
    for copy, sends in pending:

        @pl.when(sends)
        def _():
            copy.wait_send()

    for sem, size in enumerate((3 * CUT + 1, 3 * (FZ - CUT), 2 * HALF, 2 * HALF)):
        sent = chunk_a.at[pl.ds(0, (group - 1) * size)]
        pltpu.make_async_copy(sent, sent, send_sem.at[sem]).wait()


def turn_magnet(m, back_got, rows, half):
    for t in range(rows // TILE):
        for layer in range(HALF):
            z = half * HALF + layer
            places = [pl.ds((comp * FZ + z) * rows + t * TILE, TILE) for comp in range(3)]
            mx, my, mz = (m[at, :] for at in places)
            at = (half * rows + t * TILE) * 2 * HALF + 2 * layer
            u = back_got[pl.ds(at, TILE, stride=2 * HALF), :]
            v = back_got[pl.ds(at + 1, TILE, stride=2 * HALF), :]
            big_x, big_y = largest(mx, my, mz)
            big = jnp.where(big_x, mx, jnp.where(big_y, my, mz))
            mu = jnp.where(big_x, my, jnp.where(big_y, mz, mx))
            mv = jnp.where(big_x, mz, jnp.where(big_y, mx, my))
            tiny = jnp.abs(big) < 1e-30
            scale = jnp.where(tiny, 0.0, 1.0 / jnp.where(tiny, 1.0, big))
            w = -((mu * scale) * u + (mv * scale) * v)
            m[places[0], :] = mx + jnp.where(big_x, w, jnp.where(big_y, v, u))
            m[places[1], :] = my + jnp.where(big_x, u, jnp.where(big_y, w, v))
            m[places[2], :] = mz + jnp.where(big_x, v, jnp.where(big_y, u, w))


def store_kernel(rows, e, h, m, back_got, e_out, h_out, m_out, part, sem):
    size = HALF * rows
    copies = [
        pltpu.make_async_copy(src, dst, sem.at[i]) for i, (src, dst) in enumerate(((e, e_out), (h, h_out)))
    ]
    for comp in range(3):
        at = pl.ds(comp * FZ * rows, size)
        copies.append(pltpu.make_async_copy(m.at[at], m_out.at[at], sem.at[2 + comp]))
    for copy in copies:
        copy.start()
    for comp in range(3):
        part[pl.ds((comp * FZ + HALF) * rows, size), :] = m[pl.ds((comp * FZ + HALF) * rows, size), :]
    turn_magnet(part, back_got, rows, 1)
    for comp in range(3):
        at = pl.ds((comp * FZ + HALF) * rows, size)
        copy = pltpu.make_async_copy(part.at[at], m_out.at[at], sem.at[5 + comp])
        copy.start()
        copies.append(copy)
    for copy in copies:
        copy.wait()


def largest(mx, my, mz):
    sx, sy, sz = jnp.abs(mx), jnp.abs(my), jnp.abs(mz)
    big_x = (sx >= sy) & (sx >= sz)
    big_y = sy >= sz
    return big_x, big_y


def shards(efield, hfield, magnet, material, drive):
    _, nz, rows, cols_y = efield.shape
    count_x = lax.axis_size("emx")
    emy, grp = lax.axis_size("emy"), lax.axis_size("grp")
    group = emy * grp
    assert cols_y == LANES and rows == group and magnet.shape[2] == 1
    film = 3 * FZ
    tiles = rows // TILE
    assert 2 * nz * tiles <= LANES and 2 * film <= LANES
    f32 = jnp.float32
    field_shape = (3 * nz * rows, LANES)
    spin_shape = (film * group, LANES)
    dma = pltpu.SemaphoreType.DMA
    any_spec = pl.BlockSpec(memory_space=pl.ANY)
    sizes = (nz, rows, count_x, group, emy, grp)
    vmem_spec = pl.BlockSpec(memory_space=pltpu.VMEM)
    operands = [
        pltpu.with_memory_space_constraint(operand, pltpu.HBM)
        for operand in (
            efield.reshape(field_shape),
            hfield.reshape(field_shape),
            magnet.reshape(spin_shape),
            material,
            drive,
        )
    ]
    held = pl.pallas_call(
        functools.partial(step_kernel, sizes),
        out_shape=(
            pltpu.VMEM(field_shape, f32),
            pltpu.VMEM(field_shape, f32),
            pltpu.VMEM(spin_shape, f32),
            pltpu.VMEM((group * 2 * FZ, LANES), f32),
        ),
        in_specs=[any_spec] * 5,
        out_specs=[vmem_spec] * 4,
        scratch_shapes=[
            pltpu.VMEM((rows, LANES), jnp.int32),
            pltpu.VMEM((rows, LANES), f32),
            pltpu.VMEM((group * PITCH, LANES), f32),
            pltpu.VMEM((group * PITCH, LANES), f32),
            pltpu.VMEM(((rows + 2) * PITCH, LANES), f32),
            pltpu.VMEM(((rows + 2) * PITCH, LANES), f32),
            pltpu.VMEM((2 * nz, LANES), f32),
            pltpu.VMEM((2 * nz, LANES), f32),
            pltpu.VMEM((TILE, LANES), f32),
            pltpu.VMEM((TILE, LANES), f32),
            pltpu.VMEM((2 * nz, LANES), f32),
            pltpu.VMEM((2 * nz, LANES), f32),
            pltpu.VMEM((TILE, LANES), f32),
            pltpu.VMEM((TILE, LANES), f32),
            pltpu.VMEM((rows * 2 * FZ, LANES), f32),
            dma((10,)),
            pltpu.SemaphoreType.REGULAR,
            dma((4,)),
            dma((2, 4)),
            dma((2, 3)),
            dma((2, 2, 2)),
            dma((2,)),
        ],
        compiler_params=pltpu.CompilerParams(
            collective_id=0, has_side_effects=True, vmem_limit_bytes=32 * 1024 * 1024
        ),
    )(*operands)
    outs = pl.pallas_call(
        functools.partial(store_kernel, rows),
        out_shape=(
            jax.ShapeDtypeStruct(field_shape, f32),
            jax.ShapeDtypeStruct(field_shape, f32),
            jax.ShapeDtypeStruct(spin_shape, f32),
        ),
        in_specs=[vmem_spec] * 4,
        out_specs=[any_spec] * 3,
        scratch_shapes=[pltpu.VMEM(spin_shape, f32), dma((8,))],
    )(*(pltpu.with_memory_space_constraint(part, pltpu.VMEM) for part in held))
    return (
        outs[0].reshape(efield.shape),
        outs[1].reshape(hfield.shape),
        outs[2].reshape(magnet.shape),
    )


def solution(mesh):
    return jax.shard_map(
        shards,
        mesh=mesh,
        in_specs=(
            P(None, None, "emx", ("emy", "grp")),
            P(None, None, "emx", ("emy", "grp")),
            P(None, None, ("emx", "emy", "grp"), None),
            P("emx", ("emy", "grp")),
            P("emx", ("emy", "grp")),
        ),
        out_specs=(
            P(None, None, "emx", ("emy", "grp")),
            P(None, None, "emx", ("emy", "grp")),
            P(None, None, ("emx", "emy", "grp"), None),
        ),
        check_vma=False,
    )
```
